32 devices in a mesh: slab: 2 (over y), genome: 4 (over x, core), group: 4 (over z).
Axes of the slice: x: 2, y: 2, z: 4, core: 2. Of those that a mesh axis runs over, the one named last changes fastest.
Arguments:
- genotypes: bfloat16 [640, 12288], P(None, ('slab', 'genome', 'group')), parts along dimension 1, may hold values from -6 to 6
Outputs:
- ld_score: float32 [12288], P(('slab', 'genome', 'group')), parts along dimension 0
The draws below stay inside these ranges and needn't reach their ends.
There are 2 independent parts, one for each index of `slab`. The reference program is written for one: setup_inputs(seed, part) draws one part's arguments, and reference() takes and returns one part's arrays. A program takes and returns all parts, laid end to end along the dimension named above; each array names one. Nothing has to cross between parts.
All inputs are finite; a program needn't handle non-finite values.
Results may differ from the reference program's by a relative error of at most 0.0003.
Values may be sent and summed in bfloat16 or wider, within the bound.
A program may use at most 64 MiB of HBM per device.

```python
import jax
import jax.numpy as jnp
from jax import lax

SAMP = 640
PANEL = 1536
VARIANTS = 6144
N_GENOME = 4


def block_scale(stream_key, extent, shards, smallest, largest):
    factor_of = 1.0
    for position, shards_of in shards:
        draws = jax.random.uniform(jax.random.fold_in(jax.random.fold_in(stream_key, 6), position), (shards_of,), jnp.float32, smallest / len(shards), largest / len(shards))
        factor_of = factor_of * jnp.repeat(jnp.exp(draws), extent[position] // shards_of).reshape((-1,) + (1,) * (len(extent) - 1 - position))
    return factor_of


def normal_values(own_key, dims, deviation, bound, pieces=(), kind=jnp.bfloat16):
    level = block_scale(own_key, dims, pieces, -0.22, 0.18) if pieces else 1.0
    drawn = jax.random.normal(own_key, dims, jnp.float32) * deviation * level
    return jnp.minimum(jnp.maximum(drawn, -bound), bound).astype(kind)


def setup_inputs(seed: int = 0, part: int = 0) -> dict:
    keys = jax.random.split(jax.random.key(seed), 2)
    part_splits = jax.random.split(jax.random.fold_in(keys[1], part), 2)
    genotypes = normal_values(part_splits[0], (SAMP, VARIANTS), 1.0, 6.0, ((1, 16),))
    return {"genotypes": genotypes}


def reference(genotypes):
    padded = jnp.pad(genotypes, ((0, 0), (0, PANEL)))
    scaling = 1.0 / SAMP

    def one_panel(which):
        begin = (which * PANEL).astype(jnp.int32)
        row_block = lax.dynamic_slice_in_dim(genotypes, begin, PANEL, 1)
        column_block = lax.dynamic_slice_in_dim(padded, begin, 2 * PANEL, 1)
        band = jnp.dot(row_block.T, column_block, preferred_element_type=jnp.float32) * scaling
        return jnp.sum(band * band, axis=1)

    scores = lax.map(one_panel, jnp.arange(N_GENOME, dtype=jnp.int32))
    return scores.reshape(VARIANTS)
```

```python
import functools

import jax
import jax.numpy as jnp
from jax import lax
from jax.experimental import pallas as pl
from jax.experimental.pallas import tpu as pltpu
from jax.sharding import PartitionSpec as P

MESH = pl.DeviceIdType.MESH
B = 128
SKEW = 2


def plan(samples):
    blocks = [(i, j) for i in range(samples // B) for j in range(i + 1)]
    per = 3 if len(blocks) % 3 == 0 else 1
    chunks = [list(range(k, k + per)) for k in range(0, len(blocks), per)]
    return blocks, per, chunks


def pieces(blocks, chunk):
    runs = []
    for b in chunk:
        i, j = blocks[b]
        if runs and runs[-1][0] == i:
            runs[-1][3] += 1
        else:
            runs.append([i, j, b, 1])
    return runs


def kernel(
    n, ng, mine, out, following, own, from_left, from_right, to_right, to_left,
    x_send, x_recv, r_send, r_recv, l_send, l_recv,
):
    z = lax.axis_index("group")
    g = lax.axis_index("genome")
    samples, width = mine.shape
    blocks, per, chunks = plan(samples)
    rows = samples // B

    has_left, has_right = z > 0, z < n - 1
    has_before, has_next = g > 0, g < ng - 1

    barrier = pltpu.get_barrier_semaphore()

    def greet(there, where):
        @pl.when(there)
        def _():
            pl.semaphore_signal(barrier, inc=1, device_id=where, device_id_type=MESH)

    greet(has_left, {"group": z - 1})
    greet(has_right, {"group": z + 1})
    greet(has_next, {"genome": g + 1})
    peers = jnp.minimum(z, 1) + jnp.minimum(n - 1 - z, 1) + jnp.minimum(g, 1)
    pl.semaphore_wait(barrier, peers)

    def row_copy(i):
        return pltpu.make_async_remote_copy(
            src_ref=mine.at[pl.ds(i * B, B)],
            dst_ref=following.at[pl.ds(i * B, B)],
            send_sem=x_send.at[i],
            recv_sem=x_recv.at[i],
            device_id={"genome": g - 1},
            device_id_type=MESH,
        )

    def right_copy(c):
        return pltpu.make_async_remote_copy(
            src_ref=to_right.at[pl.ds(c * per, per)],
            dst_ref=from_left.at[pl.ds(c * per, per)],
            send_sem=r_send.at[c],
            recv_sem=r_recv.at[c],
            device_id={"group": z + 1},
            device_id_type=MESH,
        )

    def left_copy(c):
        return pltpu.make_async_remote_copy(
            src_ref=to_left.at[pl.ds(c * per, per)],
            dst_ref=from_right.at[pl.ds(c * per, per)],
            send_sem=l_send.at[c],
            recv_sem=l_recv.at[c],
            device_id={"group": z - 1},
            device_id_type=MESH,
        )

    @pl.when(has_before)
    def _():
        for i in range(rows):
            row_copy(i).start()

    def products(ref, run, add):
        i, j, b, count = run
        band = lax.dot_general(
            ref[pl.ds(i * B, B), :],
            ref[pl.ds(j * B, count * B), :],
            (((1,), (1,)), ((), ())),
            preferred_element_type=jnp.float32,
        )
        for k in range(count):
            block = band[:, k * B : (k + 1) * B]
            own[b + k] = own[b + k] + block if add else block

    arrived = 0
    for t in range(len(chunks) + SKEW * (n - 1)):
        if t < len(chunks):
            runs = pieces(blocks, chunks[t])
            for run in runs:
                products(mine, run, False)
            need = runs[-1][0] + 1

            @pl.when(has_next)
            def _():
                for i in range(arrived, need):
                    row_copy(i).wait_recv()
                for run in runs:
                    products(following, run, True)

            arrived = need

        c = t - SKEW * z

        @pl.when(has_right & (c >= 0) & (c < len(chunks)))
        def _():
            span = pl.ds(c * per, per)

            @pl.when(has_left)
            def _():
                right_copy(c).wait_recv()
                total = own[span] + from_left[span].astype(jnp.float32)
                to_right[span] = total.astype(to_right.dtype)

            @pl.when(z == 0)
            def _():
                to_right[span] = own[span].astype(to_right.dtype)

            right_copy(c).start()

        d = t - SKEW * (n - 1 - z)

        @pl.when(has_left & (d >= 0) & (d < len(chunks)))
        def _():
            span = pl.ds(d * per, per)

            @pl.when(has_right)
            def _():
                left_copy(d).wait_recv()
                total = own[span] + from_right[span].astype(jnp.float32)
                to_left[span] = total.astype(to_left.dtype)

            @pl.when(z == n - 1)
            def _():
                to_left[span] = own[span].astype(to_left.dtype)

            left_copy(d).start()

    score = jnp.zeros((1, width), jnp.float32)
    for c, chunk in enumerate(chunks):
        span = pl.ds(c * per, per)

        @pl.when(has_left)
        def _():
            @pl.when(z == n - 1)
            def _():
                right_copy(c).wait_recv()

            own[span] = own[span] + from_left[span].astype(jnp.float32)

        @pl.when(has_right)
        def _():
            @pl.when(z == 0)
            def _():
                left_copy(c).wait_recv()

            own[span] = own[span] + from_right[span].astype(jnp.float32)

        for i, j, b, count in pieces(blocks, chunk):
            parts = []
            for k in range(count):
                part = own[b + k]
                parts.append(part if j + k == i else part + part)
            whole = jnp.concatenate(parts, axis=1) if count > 1 else parts[0]
            high = whole.astype(jnp.bfloat16)
            low = (whole - high.astype(jnp.float32)).astype(jnp.bfloat16)
            both = lax.dot_general(
                jnp.concatenate([high, low], axis=0),
                mine[pl.ds(j * B, count * B), :],
                (((1,), (0,)), ((), ())),
                preferred_element_type=jnp.float32,
            )
            weighed = both[:B] + both[B:]
            score = score + jnp.sum(
                weighed * mine[pl.ds(i * B, B), :].astype(jnp.float32),
                axis=0,
                keepdims=True,
            )
    out[...] = score * (1.0 / samples) * (1.0 / samples)

    @pl.when(has_before)
    def _():
        for i in range(rows):
            row_copy(i).wait_send()

    @pl.when(has_right)
    def _():
        for c in range(len(chunks)):
            right_copy(c).wait_send()

    @pl.when(has_left)
    def _():
        for c in range(len(chunks)):
            left_copy(c).wait_send()


def solution(mesh):
    n, ng = mesh.shape["group"], mesh.shape["genome"]

    def per_device(genotypes):
        samples, width = genotypes.shape
        blocks, per, chunks = plan(samples)
        steps, rows = len(chunks), samples // B
        sent = pltpu.VMEM((len(blocks), B, B), jnp.bfloat16)
        scores = pl.pallas_call(
            functools.partial(kernel, n, ng),
            out_shape=jax.ShapeDtypeStruct((1, width), jnp.float32),
            in_specs=[pl.BlockSpec(memory_space=pltpu.VMEM)],
            out_specs=pl.BlockSpec(memory_space=pltpu.VMEM),
            scratch_shapes=[
                pltpu.VMEM((samples, width), jnp.bfloat16),
                pltpu.VMEM((len(blocks), B, B), jnp.float32),
                sent,
                sent,
                sent,
                sent,
                pltpu.SemaphoreType.DMA((rows,)),
                pltpu.SemaphoreType.DMA((rows,)),
                pltpu.SemaphoreType.DMA((steps,)),
                pltpu.SemaphoreType.DMA((steps,)),
                pltpu.SemaphoreType.DMA((steps,)),
                pltpu.SemaphoreType.DMA((steps,)),
            ],
            compiler_params=pltpu.CompilerParams(
                collective_id=0,
                has_side_effects=True,
                vmem_limit_bytes=32 * 1024 * 1024,
            ),
        )(genotypes)
        return scores.reshape(width)

    return jax.shard_map(
        per_device,
        mesh=mesh,
        in_specs=(P(None, ("slab", "genome", "group")),),
        out_specs=P(("slab", "genome", "group")),
        check_vma=False,
    )
```

```python
import functools

import jax
import jax.numpy as jnp
from jax import lax
from jax.experimental import pallas as pl
from jax.experimental.pallas import tpu as pltpu
from jax.sharding import PartitionSpec as P

MESH = pl.DeviceIdType.MESH
B = 128
SKEW = 3


def triangle(rows):
    return [(i, j) for i in range(rows) for j in range(i + 1)]


def kernel(
    n, ng, given, out, mine, following, own, from_left, from_right, to_right, to_left,
    m_sem, x_send, x_recv, r_send, r_recv, l_send, l_recv,
):
    z = lax.axis_index("group")
    g = lax.axis_index("genome")
    samples, width = given.shape
    rows = samples // B
    blocks = triangle(rows)
    first = [i * (i + 1) // 2 for i in range(rows)]

    has_left, has_right = z > 0, z < n - 1
    has_before, has_next = g > 0, g < ng - 1

    barrier = pltpu.get_barrier_semaphore()

    def greet(there, where):
        @pl.when(there)
        def _():
            pl.semaphore_signal(barrier, inc=1, device_id=where, device_id_type=MESH)

    greet(has_left, {"group": z - 1})
    greet(has_right, {"group": z + 1})
    greet(has_next, {"genome": g + 1})
    def load(i):
        span = pl.ds(i * B, B)
        return pltpu.make_async_copy(given.at[span], mine.at[span], m_sem.at[i])

    for i in range(rows):
        load(i).start()

    peers = jnp.minimum(z, 1) + jnp.minimum(n - 1 - z, 1) + jnp.minimum(g, 1)
    pl.semaphore_wait(barrier, peers)

    def row_copy(i):
        return pltpu.make_async_remote_copy(
            src_ref=given.at[pl.ds(i * B, B)],
            dst_ref=following.at[pl.ds(i * B, B)],
            send_sem=x_send.at[i],
            recv_sem=x_recv.at[i],
            device_id={"genome": g - 1},
            device_id_type=MESH,
        )

    def right_copy(c):
        return pltpu.make_async_remote_copy(
            src_ref=to_right.at[c],
            dst_ref=from_left.at[c],
            send_sem=r_send.at[c],
            recv_sem=r_recv.at[c],
            device_id={"group": z + 1},
            device_id_type=MESH,
        )

    def left_copy(c):
        return pltpu.make_async_remote_copy(
            src_ref=to_left.at[c],
            dst_ref=from_right.at[c],
            send_sem=l_send.at[c],
            recv_sem=l_recv.at[c],
            device_id={"group": z - 1},
            device_id_type=MESH,
        )

    @pl.when(has_before)
    def _():
        for i in range(rows):
            row_copy(i).start()

    def products(ref, i, add):
        band = lax.dot_general(
            ref[pl.ds(i * B, B), :],
            ref[pl.ds(0, (i + 1) * B), :],
            (((1,), (1,)), ((), ())),
            preferred_element_type=jnp.float32,
        )
        for j in range(i + 1):
            block = band[:, j * B : (j + 1) * B]
            own[first[i] + j] = own[first[i] + j] + block if add else block

    for i in range(rows):
        load(i).wait()
        products(mine, i, False)

    for t in range(len(blocks) + SKEW * (n - 1)):
        if t in first:
            i = first.index(t)

            @pl.when(has_next)
            def _():
                row_copy(i).wait_recv()
                products(following, i, True)

        c = t - SKEW * z

        @pl.when(has_right & (c >= 0) & (c < len(blocks)))
        def _():
            @pl.when(has_left)
            def _():
                right_copy(c).wait_recv()
                total = own[c] + from_left[c].astype(jnp.float32)
                to_right[c] = total.astype(to_right.dtype)

            @pl.when(z == 0)
            def _():
                to_right[c] = own[c].astype(to_right.dtype)

            right_copy(c).start()

        d = t - SKEW * (n - 1 - z)

        @pl.when(has_left & (d >= 0) & (d < len(blocks)))
        def _():
            @pl.when(has_right)
            def _():
                left_copy(d).wait_recv()
                total = own[d] + from_right[d].astype(jnp.float32)
                to_left[d] = total.astype(to_left.dtype)

            @pl.when(z == n - 1)
            def _():
                to_left[d] = own[d].astype(to_left.dtype)

            left_copy(d).start()

    score = jnp.zeros((1, width), jnp.float32)
    for i in range(rows):
        span = pl.ds(first[i], i + 1)

        @pl.when(has_left)
        def _():
            @pl.when(z == n - 1)
            def _():
                for j in range(i + 1):
                    right_copy(first[i] + j).wait_recv()

            own[span] = own[span] + from_left[span].astype(jnp.float32)

        @pl.when(has_right)
        def _():
            @pl.when(z == 0)
            def _():
                for j in range(i + 1):
                    left_copy(first[i] + j).wait_recv()

            own[span] = own[span] + from_right[span].astype(jnp.float32)

        parts = []
        for j in range(i + 1):
            part = own[first[i] + j]
            parts.append(part if j == i else part + part)
        whole = jnp.concatenate(parts, axis=1) if i else parts[0]
        high = whole.astype(jnp.bfloat16)
        low = (whole - high.astype(jnp.float32)).astype(jnp.bfloat16)
        both = lax.dot_general(
            jnp.concatenate([high, low], axis=0),
            mine[pl.ds(0, (i + 1) * B), :],
            (((1,), (0,)), ((), ())),
            preferred_element_type=jnp.float32,
        )
        weighed = both[:B] + both[B:]
        score = score + jnp.sum(
            weighed * mine[pl.ds(i * B, B), :].astype(jnp.float32),
            axis=0,
            keepdims=True,
        )
    out[...] = (score * (1.0 / samples) * (1.0 / samples)).reshape(width)

    @pl.when(has_before)
    def _():
        for i in range(rows):
            row_copy(i).wait_send()

    @pl.when(has_right)
    def _():
        for c in range(len(blocks)):
            right_copy(c).wait_send()

    @pl.when(has_left)
    def _():
        for c in range(len(blocks)):
            left_copy(c).wait_send()


def solution(mesh):
    n, ng = mesh.shape["group"], mesh.shape["genome"]

    def per_device(genotypes):
        samples, width = genotypes.shape
        rows = samples // B
        steps = len(triangle(rows))
        sent = pltpu.VMEM((steps, B, B), jnp.bfloat16)
        return pl.pallas_call(
            functools.partial(kernel, n, ng),
            out_shape=jax.ShapeDtypeStruct((width,), jnp.float32),
            in_specs=[pl.BlockSpec(memory_space=pl.ANY)],
            out_specs=pl.BlockSpec(memory_space=pltpu.VMEM),
            scratch_shapes=[
                pltpu.VMEM((samples, width), jnp.bfloat16),
                pltpu.VMEM((samples, width), jnp.bfloat16),
                pltpu.VMEM((steps, B, B), jnp.float32),
                sent,
                sent,
                sent,
                sent,
                pltpu.SemaphoreType.DMA((rows,)),
                pltpu.SemaphoreType.DMA((rows,)),
                pltpu.SemaphoreType.DMA((rows,)),
                pltpu.SemaphoreType.DMA((steps,)),
                pltpu.SemaphoreType.DMA((steps,)),
                pltpu.SemaphoreType.DMA((steps,)),
                pltpu.SemaphoreType.DMA((steps,)),
            ],
            compiler_params=pltpu.CompilerParams(
                collective_id=0,
                has_side_effects=True,
                vmem_limit_bytes=63 * 1024 * 1024,
            ),
        )(genotypes)

    return jax.shard_map(
        per_device,
        mesh=mesh,
        in_specs=(P(None, ("slab", "genome", "group")),),
        out_specs=P(("slab", "genome", "group")),
        check_vma=False,
    )
```

```python
import functools

import jax
import jax.numpy as jnp
from jax import lax
from jax.experimental import pallas as pl
from jax.experimental.pallas import tpu as pltpu
from jax.sharding import PartitionSpec as P

MESH = pl.DeviceIdType.MESH
B = 128
SKEW = 3
LAG = 3


def triangle(rows):
    return [(i, j) for i in range(rows) for j in range(i + 1)]


def kernel(
    n, ng, given, out, mine, following, own, from_left, from_right, to_right, to_left,
    from_next, to_before, m_sem, x_send, x_recv, s_send, s_recv, r_send, r_recv, l_send, l_recv,
):
    z = lax.axis_index("group")
    g = lax.axis_index("genome")
    samples, width = given.shape
    rows = samples // B
    blocks = triangle(rows)
    first = [i * (i + 1) // 2 for i in range(rows)]
    late = rows - 1

    has_left, has_right = z > 0, z < n - 1
    has_before, has_next = g > 0, g < ng - 1

    barrier = pltpu.get_barrier_semaphore()

    def greet(there, where):
        @pl.when(there)
        def _():
            pl.semaphore_signal(barrier, inc=1, device_id=where, device_id_type=MESH)

    greet(has_left, {"group": z - 1})
    greet(has_right, {"group": z + 1})
    greet(has_next, {"genome": g + 1})
    def load(i):
        span = pl.ds(i * B, B)
        return pltpu.make_async_copy(given.at[span], mine.at[span], m_sem.at[i])

    for i in range(rows):
        load(i).start()

    peers = jnp.minimum(z, 1) + jnp.minimum(n - 1 - z, 1) + jnp.minimum(g, 1)
    pl.semaphore_wait(barrier, peers)

    def slice_copy():
        return pltpu.make_async_remote_copy(
            src_ref=mine,
            dst_ref=following,
            send_sem=x_send,
            recv_sem=x_recv,
            device_id={"genome": g - 1},
            device_id_type=MESH,
        )

    def sum_copy(c):
        return pltpu.make_async_remote_copy(
            src_ref=to_before.at[c],
            dst_ref=from_next.at[c],
            send_sem=s_send.at[c],
            recv_sem=s_recv.at[c],
            device_id={"genome": g - 1},
            device_id_type=MESH,
        )

    def right_copy(c):
        return pltpu.make_async_remote_copy(
            src_ref=to_right.at[c],
            dst_ref=from_left.at[c],
            send_sem=r_send.at[c],
            recv_sem=r_recv.at[c],
            device_id={"group": z + 1},
            device_id_type=MESH,
        )

    def left_copy(c):
        return pltpu.make_async_remote_copy(
            src_ref=to_left.at[c],
            dst_ref=from_right.at[c],
            send_sem=l_send.at[c],
            recv_sem=l_recv.at[c],
            device_id={"group": z - 1},
            device_id_type=MESH,
        )

    def products(ref, i, add):
        band = lax.dot_general(
            ref[pl.ds(i * B, B), :],
            ref[pl.ds(0, (i + 1) * B), :],
            (((1,), (1,)), ((), ())),
            preferred_element_type=jnp.float32,
        )
        for j in range(i + 1):
            block = band[:, j * B : (j + 1) * B]
            own[first[i] + j] = own[first[i] + j] + block if add else block

    score = jnp.zeros((1, width), jnp.float32)

    def scored(score, i):
        span = pl.ds(first[i], i + 1)
        if i < late:

            @pl.when(has_next)
            def _():
                for j in range(i + 1):
                    sum_copy(first[i] + j).wait_recv()
                own[span] = own[span] + from_next[span].astype(jnp.float32)

        parts = []
        for j in range(i + 1):
            part = own[first[i] + j]
            parts.append(part if j == i else part + part)
        whole = jnp.concatenate(parts, axis=1) if i else parts[0]
        high = whole.astype(jnp.bfloat16)
        low = (whole - high.astype(jnp.float32)).astype(jnp.bfloat16)
        both = lax.dot_general(
            jnp.concatenate([high, low], axis=0),
            mine[pl.ds(0, (i + 1) * B), :],
            (((1,), (0,)), ((), ())),
            preferred_element_type=jnp.float32,
        )
        weighed = both[:B] + both[B:]
        return score + jnp.sum(
            weighed * mine[pl.ds(i * B, B), :].astype(jnp.float32),
            axis=0,
            keepdims=True,
        )

    load(0).wait()
    products(mine, 0, False)

    for t in range(len(blocks) + SKEW * (n - 1)):
        if t == first[late]:

            @pl.when(has_next)
            def _():
                slice_copy().wait_recv()
                products(following, late, True)

        c = t - SKEW * z

        @pl.when(has_right & (c >= 0) & (c < len(blocks)))
        def _():
            @pl.when(has_left)
            def _():
                right_copy(c).wait_recv()
                total = own[c] + from_left[c].astype(jnp.float32)
                to_right[c] = total.astype(to_right.dtype)

            @pl.when(z == 0)
            def _():
                to_right[c] = own[c].astype(to_right.dtype)

            right_copy(c).start()

        d = t - SKEW * (n - 1 - z)

        @pl.when(has_left & (d >= 0) & (d < len(blocks)))
        def _():
            @pl.when(has_right)
            def _():
                left_copy(d).wait_recv()
                total = own[d] + from_right[d].astype(jnp.float32)
                to_left[d] = total.astype(to_left.dtype)

            @pl.when(z == n - 1)
            def _():
                to_left[d] = own[d].astype(to_left.dtype)

            left_copy(d).start()

        if t == 0:
            for i in range(1, rows):
                load(i).wait()

            @pl.when(has_before)
            def _():
                slice_copy().start()

        if t in first[: rows - 1]:
            products(mine, first.index(t) + 1, False)

        f = t - SKEW * jnp.maximum(z, n - 1 - z)

        @pl.when((f >= 0) & (f < len(blocks)))
        def _():
            @pl.when(has_left)
            def _():
                @pl.when(z == n - 1)
                def _():
                    right_copy(f).wait_recv()

                own[f] = own[f] + from_left[f].astype(jnp.float32)

            @pl.when(has_right)
            def _():
                @pl.when(z == 0)
                def _():
                    left_copy(f).wait_recv()

                own[f] = own[f] + from_right[f].astype(jnp.float32)

            @pl.when(has_before & (f < first[late]))
            def _():
                to_before[f] = own[f].astype(to_before.dtype)
                sum_copy(f).start()

        ready = t - LAG - SKEW * (n - 1)
        for i in range(late):
            if ready == first[i] + i:
                score = scored(score, i)

    for i in range(late, rows):
        score = scored(score, i)
    out[...] = score * (1.0 / samples) * (1.0 / samples)

    @pl.when(has_before)
    def _():
        slice_copy().wait_send()
        for c in range(first[late]):
            sum_copy(c).wait_send()

    @pl.when(has_right)
    def _():
        for c in range(len(blocks)):
            right_copy(c).wait_send()

    @pl.when(has_left)
    def _():
        for c in range(len(blocks)):
            left_copy(c).wait_send()


def solution(mesh):
    n, ng = mesh.shape["group"], mesh.shape["genome"]

    def per_device(genotypes):
        samples, width = genotypes.shape
        rows = samples // B
        steps = len(triangle(rows))
        sent = pltpu.VMEM((steps, B, B), jnp.bfloat16)
        scores = pl.pallas_call(
            functools.partial(kernel, n, ng),
            out_shape=jax.ShapeDtypeStruct((1, width), jnp.float32),
            in_specs=[pl.BlockSpec(memory_space=pl.ANY)],
            out_specs=pl.BlockSpec(memory_space=pltpu.VMEM),
            scratch_shapes=[
                pltpu.VMEM((samples, width), jnp.bfloat16),
                pltpu.VMEM((samples, width), jnp.bfloat16),
                pltpu.VMEM((steps, B, B), jnp.float32),
                sent,
                sent,
                sent,
                sent,
                sent,
                sent,
                pltpu.SemaphoreType.DMA((rows,)),
                pltpu.SemaphoreType.DMA,
                pltpu.SemaphoreType.DMA,
                pltpu.SemaphoreType.DMA((steps,)),
                pltpu.SemaphoreType.DMA((steps,)),
                pltpu.SemaphoreType.DMA((steps,)),
                pltpu.SemaphoreType.DMA((steps,)),
                pltpu.SemaphoreType.DMA((steps,)),
                pltpu.SemaphoreType.DMA((steps,)),
            ],
            compiler_params=pltpu.CompilerParams(
                collective_id=0,
                has_side_effects=True,
                vmem_limit_bytes=63 * 1024 * 1024,
            ),
        )(genotypes)
        return scores.reshape(width)

    return jax.shard_map(
        per_device,
        mesh=mesh,
        in_specs=(P(None, ("slab", "genome", "group")),),
        out_specs=P(("slab", "genome", "group")),
        check_vma=False,
    )
```

```python
import functools

import jax
import jax.numpy as jnp
from jax import lax
from jax.experimental import pallas as pl
from jax.experimental.pallas import tpu as pltpu
from jax.sharding import PartitionSpec as P

MESH = pl.DeviceIdType.MESH
B = 128
SKEW = 2
LAG = 1


def plan(samples):
    blocks = [(i, j) for i in range(samples // B) for j in range(i + 1)]
    per = 3 if len(blocks) % 3 == 0 else 1
    chunks = [list(range(k, k + per)) for k in range(0, len(blocks), per)]
    return blocks, per, chunks


def pieces(blocks, chunk):
    runs = []
    for b in chunk:
        i, j = blocks[b]
        if runs and runs[-1][0] == i:
            runs[-1][3] += 1
        else:
            runs.append([i, j, b, 1])
    return runs


def kernel(
    n, ng, given, out, mine, own, from_left, from_right, to_right, to_left,
    from_next, to_before, m_sem, s_send, s_recv, r_send, r_recv, l_send, l_recv,
):
    z = lax.axis_index("group")
    g = lax.axis_index("genome")
    samples, width = given.shape
    rows = samples // B
    blocks, per, chunks = plan(samples)
    steps = len(chunks)

    has_left, has_right = z > 0, z < n - 1
    has_before, has_next = g > 0, g < ng - 1

    barrier = pltpu.get_barrier_semaphore()

    def greet(there, where):
        @pl.when(there)
        def _():
            pl.semaphore_signal(barrier, inc=1, device_id=where, device_id_type=MESH)

    greet(has_left, {"group": z - 1})
    greet(has_right, {"group": z + 1})
    greet(has_next, {"genome": g + 1})
    def load(i):
        span = pl.ds(i * B, B)
        return pltpu.make_async_copy(given.at[span], mine.at[span], m_sem.at[i])

    for i in range(rows):
        load(i).start()

    peers = jnp.minimum(z, 1) + jnp.minimum(n - 1 - z, 1) + jnp.minimum(g, 1)
    pl.semaphore_wait(barrier, peers)

    def sum_copy(c):
        return pltpu.make_async_remote_copy(
            src_ref=to_before.at[pl.ds(c * per, per)],
            dst_ref=from_next.at[pl.ds(c * per, per)],
            send_sem=s_send.at[c],
            recv_sem=s_recv.at[c],
            device_id={"genome": g - 1},
            device_id_type=MESH,
        )

    def right_copy(c):
        return pltpu.make_async_remote_copy(
            src_ref=to_right.at[pl.ds(c * per, per)],
            dst_ref=from_left.at[pl.ds(c * per, per)],
            send_sem=r_send.at[c],
            recv_sem=r_recv.at[c],
            device_id={"group": z + 1},
            device_id_type=MESH,
        )

    def left_copy(c):
        return pltpu.make_async_remote_copy(
            src_ref=to_left.at[pl.ds(c * per, per)],
            dst_ref=from_right.at[pl.ds(c * per, per)],
            send_sem=l_send.at[c],
            recv_sem=l_recv.at[c],
            device_id={"group": z - 1},
            device_id_type=MESH,
        )

    def products(chunk):
        for i, j, b, count in pieces(blocks, chunk):
            band = lax.dot_general(
                mine[pl.ds(i * B, B), :],
                mine[pl.ds(j * B, count * B), :],
                (((1,), (1,)), ((), ())),
                preferred_element_type=jnp.float32,
            )
            for k in range(count):
                own[b + k] = band[:, k * B : (k + 1) * B]

    def scored(score, c):
        span = pl.ds(c * per, per)

        @pl.when(has_next)
        def _():
            sum_copy(c).wait_recv()
            own[span] = own[span] + from_next[span].astype(jnp.float32)

        for i, j, b, count in pieces(blocks, chunks[c]):
            parts = []
            for k in range(count):
                part = own[b + k]
                parts.append(part if j + k == i else part + part)
            whole = jnp.concatenate(parts, axis=1) if count > 1 else parts[0]
            high = whole.astype(jnp.bfloat16)
            low = (whole - high.astype(jnp.float32)).astype(jnp.bfloat16)
            both = lax.dot_general(
                jnp.concatenate([high, low], axis=0),
                mine[pl.ds(j * B, count * B), :],
                (((1,), (0,)), ((), ())),
                preferred_element_type=jnp.float32,
            )
            weighed = both[:B] + both[B:]
            score = score + jnp.sum(
                weighed * mine[pl.ds(i * B, B), :].astype(jnp.float32),
                axis=0,
                keepdims=True,
            )
        return score

    score = jnp.zeros((1, width), jnp.float32)
    loaded = 0
    for t in range(-1, steps + SKEW * (n - 1)):
        c = t - SKEW * z

        @pl.when(has_right & (c >= 0) & (c < steps))
        def _():
            span = pl.ds(c * per, per)

            @pl.when(has_left)
            def _():
                right_copy(c).wait_recv()
                total = own[span] + from_left[span].astype(jnp.float32)
                to_right[span] = total.astype(to_right.dtype)

            @pl.when(z == 0)
            def _():
                to_right[span] = own[span].astype(to_right.dtype)

            right_copy(c).start()

        d = t - SKEW * (n - 1 - z)

        @pl.when(has_left & (d >= 0) & (d < steps))
        def _():
            span = pl.ds(d * per, per)

            @pl.when(has_right)
            def _():
                left_copy(d).wait_recv()
                total = own[span] + from_right[span].astype(jnp.float32)
                to_left[span] = total.astype(to_left.dtype)

            @pl.when(z == n - 1)
            def _():
                to_left[span] = own[span].astype(to_left.dtype)

            left_copy(d).start()

        if t + 1 < steps:
            need = blocks[chunks[t + 1][-1]][0] + 1
            for i in range(loaded, need):
                load(i).wait()
            loaded = need
            products(chunks[t + 1])

        f = t - SKEW * jnp.maximum(z, n - 1 - z)

        @pl.when((f >= 0) & (f < steps))
        def _():
            span = pl.ds(f * per, per)

            @pl.when(has_left)
            def _():
                @pl.when(z == n - 1)
                def _():
                    right_copy(f).wait_recv()

                own[span] = own[span] + from_left[span].astype(jnp.float32)

            @pl.when(has_right)
            def _():
                @pl.when(z == 0)
                def _():
                    left_copy(f).wait_recv()

                own[span] = own[span] + from_right[span].astype(jnp.float32)

            @pl.when(has_before)
            def _():
                to_before[span] = own[span].astype(to_before.dtype)
                sum_copy(f).start()

        ready = t - LAG - SKEW * (n - 1)
        if ready >= 0:
            score = scored(score, ready)

    for c in range(steps - LAG, steps):
        score = scored(score, c)
    out[...] = score * (1.0 / samples) * (1.0 / samples)

    @pl.when(has_before)
    def _():
        for c in range(steps):
            sum_copy(c).wait_send()

    @pl.when(has_right)
    def _():
        for c in range(steps):
            right_copy(c).wait_send()

    @pl.when(has_left)
    def _():
        for c in range(steps):
            left_copy(c).wait_send()


def solution(mesh):
    n, ng = mesh.shape["group"], mesh.shape["genome"]

    def per_device(genotypes):
        samples, width = genotypes.shape
        blocks, per, chunks = plan(samples)
        steps = len(chunks)
        sent = pltpu.VMEM((len(blocks), B, B), jnp.bfloat16)
        scores = pl.pallas_call(
            functools.partial(kernel, n, ng),
            out_shape=jax.ShapeDtypeStruct((1, width), jnp.float32),
            in_specs=[pl.BlockSpec(memory_space=pl.ANY)],
            out_specs=pl.BlockSpec(memory_space=pltpu.VMEM),
            scratch_shapes=[
                pltpu.VMEM((samples, width), jnp.bfloat16),
                pltpu.VMEM((len(blocks), B, B), jnp.float32),
                sent,
                sent,
                sent,
                sent,
                sent,
                sent,
                pltpu.SemaphoreType.DMA((samples // B,)),
                pltpu.SemaphoreType.DMA((steps,)),
                pltpu.SemaphoreType.DMA((steps,)),
                pltpu.SemaphoreType.DMA((steps,)),
                pltpu.SemaphoreType.DMA((steps,)),
                pltpu.SemaphoreType.DMA((steps,)),
                pltpu.SemaphoreType.DMA((steps,)),
            ],
            compiler_params=pltpu.CompilerParams(
                collective_id=0,
                has_side_effects=True,
                vmem_limit_bytes=63 * 1024 * 1024,
            ),
        )(genotypes)
        return scores.reshape(width)

    return jax.shard_map(
        per_device,
        mesh=mesh,
        in_specs=(P(None, ("slab", "genome", "group")),),
        out_specs=P(("slab", "genome", "group")),
        check_vma=False,
    )
```

```python
import functools

import jax
import jax.numpy as jnp
from jax import lax
from jax.experimental import pallas as pl
from jax.experimental.pallas import tpu as pltpu
from jax.sharding import PartitionSpec as P

MESH = pl.DeviceIdType.MESH
B = 128
SKEW = 3
LAG = 6


def triangle(rows):
    return [(i, j) for i in range(rows) for j in range(i + 1)]


def kernel(
    n, ng, given, out, mine, following, own, from_left, from_right, to_right, to_left,
    from_next, to_before, m_sem, x_send, x_recv, s_send, s_recv, r_send, r_recv, l_send, l_recv,
):
    z = lax.axis_index("group")
    g = lax.axis_index("genome")
    samples, width = given.shape
    rows = samples // B
    blocks = triangle(rows)
    first = [i * (i + 1) // 2 for i in range(rows)]
    late = rows - 1

    has_left, has_right = z > 0, z < n - 1
    has_before, has_next = g > 0, g < ng - 1

    barrier = pltpu.get_barrier_semaphore()

    def greet(there, where):
        @pl.when(there)
        def _():
            pl.semaphore_signal(barrier, inc=1, device_id=where, device_id_type=MESH)

    greet(has_left, {"group": z - 1})
    greet(has_right, {"group": z + 1})
    greet(has_next, {"genome": g + 1})
    def load(i):
        span = pl.ds(i * B, B)
        return pltpu.make_async_copy(given.at[span], mine.at[span], m_sem.at[i])

    for i in range(rows):
        load(i).start()

    peers = jnp.minimum(z, 1) + jnp.minimum(n - 1 - z, 1) + jnp.minimum(g, 1)
    pl.semaphore_wait(barrier, peers)

    def row_copy(i):
        span = pl.ds(i * B, B)
        return pltpu.make_async_remote_copy(
            src_ref=mine.at[span],
            dst_ref=following.at[span],
            send_sem=x_send.at[i],
            recv_sem=x_recv.at[i],
            device_id={"genome": g - 1},
            device_id_type=MESH,
        )

    def sum_copy(c):
        return pltpu.make_async_remote_copy(
            src_ref=to_before.at[c],
            dst_ref=from_next.at[c],
            send_sem=s_send.at[c],
            recv_sem=s_recv.at[c],
            device_id={"genome": g - 1},
            device_id_type=MESH,
        )

    def right_copy(c):
        return pltpu.make_async_remote_copy(
            src_ref=to_right.at[c],
            dst_ref=from_left.at[c],
            send_sem=r_send.at[c],
            recv_sem=r_recv.at[c],
            device_id={"group": z + 1},
            device_id_type=MESH,
        )

    def left_copy(c):
        return pltpu.make_async_remote_copy(
            src_ref=to_left.at[c],
            dst_ref=from_right.at[c],
            send_sem=l_send.at[c],
            recv_sem=l_recv.at[c],
            device_id={"group": z - 1},
            device_id_type=MESH,
        )

    def products(ref, i, add):
        band = lax.dot_general(
            ref[pl.ds(i * B, B), :],
            ref[pl.ds(0, (i + 1) * B), :],
            (((1,), (1,)), ((), ())),
            preferred_element_type=jnp.float32,
        )
        for j in range(i + 1):
            block = band[:, j * B : (j + 1) * B]
            own[first[i] + j] = own[first[i] + j] + block if add else block

    score = jnp.zeros((1, width), jnp.float32)

    def scored(score, i):
        span = pl.ds(first[i], i + 1)
        if i < late:

            @pl.when(has_next)
            def _():
                for j in range(i + 1):
                    sum_copy(first[i] + j).wait_recv()
                own[span] = own[span] + from_next[span].astype(jnp.float32)

        parts = []
        for j in range(i + 1):
            part = own[first[i] + j]
            parts.append(part if j == i else part + part)
        whole = jnp.concatenate(parts, axis=1) if i else parts[0]
        high = whole.astype(jnp.bfloat16)
        low = (whole - high.astype(jnp.float32)).astype(jnp.bfloat16)
        both = lax.dot_general(
            jnp.concatenate([high, low], axis=0),
            mine[pl.ds(0, (i + 1) * B), :],
            (((1,), (0,)), ((), ())),
            preferred_element_type=jnp.float32,
        )
        weighed = both[:B] + both[B:]
        return score + jnp.sum(
            weighed * mine[pl.ds(i * B, B), :].astype(jnp.float32),
            axis=0,
            keepdims=True,
        )

    for i in range(rows):
        load(i).wait()

    @pl.when(has_before)
    def _():
        for i in range(rows):
            row_copy(i).start()

    products(mine, 0, False)
    pending = list(range(rows))

    for t in range(len(blocks) + SKEW * (n - 1)):
        if t == first[late]:

            @pl.when(has_next)
            def _():
                for i in range(rows):
                    row_copy(i).wait_recv()
                products(following, late, True)

        c = t - SKEW * z

        @pl.when(has_right & (c >= 0) & (c < len(blocks)))
        def _():
            @pl.when(has_left)
            def _():
                right_copy(c).wait_recv()
                total = own[c] + from_left[c].astype(jnp.float32)
                to_right[c] = total.astype(to_right.dtype)

            @pl.when(z == 0)
            def _():
                to_right[c] = own[c].astype(to_right.dtype)

            right_copy(c).start()

        d = t - SKEW * (n - 1 - z)

        @pl.when(has_left & (d >= 0) & (d < len(blocks)))
        def _():
            @pl.when(has_right)
            def _():
                left_copy(d).wait_recv()
                total = own[d] + from_right[d].astype(jnp.float32)
                to_left[d] = total.astype(to_left.dtype)

            @pl.when(z == n - 1)
            def _():
                to_left[d] = own[d].astype(to_left.dtype)

            left_copy(d).start()

        if t in first[: rows - 1]:
            products(mine, first.index(t) + 1, False)

        f = t - SKEW * jnp.maximum(z, n - 1 - z)

        @pl.when((f >= 0) & (f < len(blocks)))
        def _():
            @pl.when(has_left)
            def _():
                @pl.when(z == n - 1)
                def _():
                    right_copy(f).wait_recv()

                own[f] = own[f] + from_left[f].astype(jnp.float32)

            @pl.when(has_right)
            def _():
                @pl.when(z == 0)
                def _():
                    left_copy(f).wait_recv()

                own[f] = own[f] + from_right[f].astype(jnp.float32)

            @pl.when(has_before & (f < first[late]))
            def _():
                to_before[f] = own[f].astype(to_before.dtype)
                sum_copy(f).start()

        ready = t - LAG - SKEW * (n - 1)
        if pending[0] < late and ready == first[pending[0]] + pending[0]:
            score = scored(score, pending.pop(0))

    for i in pending:
        score = scored(score, i)
    out[...] = score * (1.0 / samples) * (1.0 / samples)

    @pl.when(has_before)
    def _():
        for i in range(rows):
            row_copy(i).wait_send()
        for c in range(first[late]):
            sum_copy(c).wait_send()

    @pl.when(has_right)
    def _():
        for c in range(len(blocks)):
            right_copy(c).wait_send()

    @pl.when(has_left)
    def _():
        for c in range(len(blocks)):
            left_copy(c).wait_send()


def solution(mesh):
    n, ng = mesh.shape["group"], mesh.shape["genome"]

    def per_device(genotypes):
        samples, width = genotypes.shape
        rows = samples // B
        steps = len(triangle(rows))
        sent = pltpu.VMEM((steps, B, B), jnp.bfloat16)
        scores = pl.pallas_call(
            functools.partial(kernel, n, ng),
            out_shape=jax.ShapeDtypeStruct((1, width), jnp.float32),
            in_specs=[pl.BlockSpec(memory_space=pl.ANY)],
            out_specs=pl.BlockSpec(memory_space=pltpu.VMEM),
            scratch_shapes=[
                pltpu.VMEM((samples, width), jnp.bfloat16),
                pltpu.VMEM((samples, width), jnp.bfloat16),
                pltpu.VMEM((steps, B, B), jnp.float32),
                sent,
                sent,
                sent,
                sent,
                sent,
                sent,
                pltpu.SemaphoreType.DMA((rows,)),
                pltpu.SemaphoreType.DMA((rows,)),
                pltpu.SemaphoreType.DMA((rows,)),
                pltpu.SemaphoreType.DMA((steps,)),
                pltpu.SemaphoreType.DMA((steps,)),
                pltpu.SemaphoreType.DMA((steps,)),
                pltpu.SemaphoreType.DMA((steps,)),
                pltpu.SemaphoreType.DMA((steps,)),
                pltpu.SemaphoreType.DMA((steps,)),
            ],
            compiler_params=pltpu.CompilerParams(
                collective_id=0,
                has_side_effects=True,
                vmem_limit_bytes=63 * 1024 * 1024,
            ),
        )(genotypes)
        return scores.reshape(width)

    return jax.shard_map(
        per_device,
        mesh=mesh,
        in_specs=(P(None, ("slab", "genome", "group")),),
        out_specs=P(("slab", "genome", "group")),
        check_vma=False,
    )
```

```python
import functools

import jax
import jax.numpy as jnp
from jax import lax
from jax.experimental import pallas as pl
from jax.experimental.pallas import tpu as pltpu
from jax.sharding import PartitionSpec as P

MESH = pl.DeviceIdType.MESH
B = 128
SKEW = 4


def triangle(rows):
    return [(i, j) for i in range(rows) for j in range(i + 1)]


def kernel(
    n, ng, given, out, mine, before, own, from_left, from_right, to_right, to_left,
    kept, to_before, from_next, m_sem, x_send, x_recv, s_send, s_recv,
    r_send, r_recv, l_send, l_recv,
):
    z = lax.axis_index("group")
    g = lax.axis_index("genome")
    samples, width = given.shape
    rows = samples // B
    blocks = triangle(rows)
    first = [i * (i + 1) // 2 for i in range(rows)]
    groups = [(i, 0, i + 1) for i in range(rows - 1)]
    groups += [(rows - 1, 0, rows - 2), (rows - 1, rows - 2, 2)]

    has_left, has_right = z > 0, z < n - 1
    has_before, has_next = g > 0, g < ng - 1

    barrier = pltpu.get_barrier_semaphore()

    def greet(there, where):
        @pl.when(there)
        def _():
            pl.semaphore_signal(barrier, inc=1, device_id=where, device_id_type=MESH)

    greet(has_left, {"group": z - 1})
    greet(has_right, {"group": z + 1})
    greet(has_before, {"genome": g - 1})
    greet(has_next, {"genome": g + 1})

    def load(i):
        span = pl.ds(i * B, B)
        return pltpu.make_async_copy(given.at[span], mine.at[span], m_sem.at[i])

    for i in range(rows):
        load(i).start()

    peers = jnp.minimum(z, 1) + jnp.minimum(n - 1 - z, 1)
    peers = peers + jnp.minimum(g, 1) + jnp.minimum(ng - 1 - g, 1)
    pl.semaphore_wait(barrier, peers)

    def row_copy(i):
        span = pl.ds(i * B, B)
        return pltpu.make_async_remote_copy(
            src_ref=mine.at[span],
            dst_ref=before.at[span],
            send_sem=x_send.at[i],
            recv_sem=x_recv.at[i],
            device_id={"genome": g + 1},
            device_id_type=MESH,
        )

    def score_copy():
        return pltpu.make_async_remote_copy(
            src_ref=to_before,
            dst_ref=from_next,
            send_sem=s_send,
            recv_sem=s_recv,
            device_id={"genome": g - 1},
            device_id_type=MESH,
        )

    def right_copy(c):
        return pltpu.make_async_remote_copy(
            src_ref=to_right.at[c],
            dst_ref=from_left.at[c],
            send_sem=r_send.at[c],
            recv_sem=r_recv.at[c],
            device_id={"group": z + 1},
            device_id_type=MESH,
        )

    def left_copy(c):
        return pltpu.make_async_remote_copy(
            src_ref=to_left.at[c],
            dst_ref=from_right.at[c],
            send_sem=l_send.at[c],
            recv_sem=l_recv.at[c],
            device_id={"group": z - 1},
            device_id_type=MESH,
        )

    def products(i):
        band = lax.dot_general(
            mine[pl.ds(i * B, B), :],
            mine[pl.ds(0, (i + 1) * B), :],
            (((1,), (1,)), ((), ())),
            preferred_element_type=jnp.float32,
        )
        for j in range(i + 1):
            own[first[i] + j] = band[:, j * B : (j + 1) * B]

    def scored(group):
        i, j, count = group
        parts = []
        for k in range(j, j + count):
            part = own[first[i] + k]
            parts.append(part if k == i else part + part)
        whole = jnp.concatenate(parts, axis=1) if count > 1 else parts[0]
        high = whole.astype(jnp.bfloat16)
        low = (whole - high.astype(jnp.float32)).astype(jnp.bfloat16)
        both = jnp.concatenate([high, low], axis=0)

        def add(total, ref):
            product = lax.dot_general(
                both,
                ref[pl.ds(j * B, count * B), :],
                (((1,), (0,)), ((), ())),
                preferred_element_type=jnp.float32,
            )
            weighed = (product[:B] + product[B:]) * ref[pl.ds(i * B, B), :].astype(
                jnp.float32
            )
            total[...] += jnp.sum(weighed, axis=0, keepdims=True)

        @pl.when(has_before)
        def _():
            if group == groups[0]:
                for k in range(rows):
                    row_copy(k).wait_recv()
            add(to_before, before)

        add(kept, mine)

    for i in range(rows):
        load(i).wait()

    products(0)
    kept[...] = jnp.zeros_like(kept)
    to_before[...] = jnp.zeros_like(to_before)
    pending = list(groups)
    at_end = (z == 0) | (z == n - 1)

    for t in range(len(blocks) + SKEW * (n - 1)):
        c = t - SKEW * z

        @pl.when(has_right & (c >= 0) & (c < len(blocks)))
        def _():
            @pl.when(has_left)
            def _():
                right_copy(c).wait_recv()
                total = own[c] + from_left[c].astype(jnp.float32)
                to_right[c] = total.astype(to_right.dtype)

            @pl.when(z == 0)
            def _():
                to_right[c] = own[c].astype(to_right.dtype)

            right_copy(c).start()

        d = t - SKEW * (n - 1 - z)

        @pl.when(has_left & (d >= 0) & (d < len(blocks)))
        def _():
            @pl.when(has_right)
            def _():
                left_copy(d).wait_recv()
                total = own[d] + from_right[d].astype(jnp.float32)
                to_left[d] = total.astype(to_left.dtype)

            @pl.when(z == n - 1)
            def _():
                to_left[d] = own[d].astype(to_left.dtype)

            left_copy(d).start()

        if t in first[: rows - 1]:
            products(first.index(t) + 1)

        if t == 1:

            @pl.when(has_next)
            def _():
                for i in range(rows):
                    row_copy(i).start()

        f = t - SKEW * jnp.maximum(z, n - 1 - z)

        @pl.when((f >= 0) & (f < len(blocks)))
        def _():
            @pl.when(has_left)
            def _():
                @pl.when(z == n - 1)
                def _():
                    right_copy(f).wait_recv()

                own[f] = own[f] + from_left[f].astype(jnp.float32)

            @pl.when(has_right)
            def _():
                @pl.when(z == 0)
                def _():
                    left_copy(f).wait_recv()

                own[f] = own[f] + from_right[f].astype(jnp.float32)

        ready = t - SKEW * (n - 1)
        group = pending[0]
        if ready == first[group[0]] + group[1] + group[2] - 1:

            @pl.when(at_end)
            def _():
                scored(group)

            pending.pop(0)

    @pl.when(jnp.logical_not(at_end))
    def _():
        for group in groups:
            scored(group)

    @pl.when(has_before)
    def _():
        score_copy().start()

    @pl.when(has_next)
    def _():
        score_copy().wait_recv()
        kept[...] += from_next[...]

    out[...] = kept[...] * (1.0 / samples) * (1.0 / samples)

    @pl.when(has_next)
    def _():
        for i in range(rows):
            row_copy(i).wait_send()

    @pl.when(has_before)
    def _():
        score_copy().wait_send()

    @pl.when(has_right)
    def _():
        for c in range(len(blocks)):
            right_copy(c).wait_send()

    @pl.when(has_left)
    def _():
        for c in range(len(blocks)):
            left_copy(c).wait_send()


def solution(mesh):
    n, ng = mesh.shape["group"], mesh.shape["genome"]

    def per_device(genotypes):
        samples, width = genotypes.shape
        rows = samples // B
        steps = len(triangle(rows))
        sent = pltpu.VMEM((steps, B, B), jnp.bfloat16)
        line = pltpu.VMEM((1, width), jnp.float32)
        scores = pl.pallas_call(
            functools.partial(kernel, n, ng),
            out_shape=jax.ShapeDtypeStruct((1, width), jnp.float32),
            in_specs=[pl.BlockSpec(memory_space=pl.ANY)],
            out_specs=pl.BlockSpec(memory_space=pltpu.VMEM),
            scratch_shapes=[
                pltpu.VMEM((samples, width), jnp.bfloat16),
                pltpu.VMEM((samples, width), jnp.bfloat16),
                pltpu.VMEM((steps, B, B), jnp.float32),
                sent,
                sent,
                sent,
                sent,
                line,
                line,
                line,
                pltpu.SemaphoreType.DMA((rows,)),
                pltpu.SemaphoreType.DMA((rows,)),
                pltpu.SemaphoreType.DMA((rows,)),
                pltpu.SemaphoreType.DMA,
                pltpu.SemaphoreType.DMA,
                pltpu.SemaphoreType.DMA((steps,)),
                pltpu.SemaphoreType.DMA((steps,)),
                pltpu.SemaphoreType.DMA((steps,)),
                pltpu.SemaphoreType.DMA((steps,)),
            ],
            compiler_params=pltpu.CompilerParams(
                collective_id=0,
                has_side_effects=True,
                vmem_limit_bytes=54784 * 1024,
            ),
        )(genotypes)
        return scores.reshape(width)

    return jax.shard_map(
        per_device,
        mesh=mesh,
        in_specs=(P(None, ("slab", "genome", "group")),),
        out_specs=P(("slab", "genome", "group")),
        check_vma=False,
    )
```

```python
import functools

import jax
import jax.numpy as jnp
from jax import lax
from jax.experimental import pallas as pl
from jax.experimental.pallas import tpu as pltpu
from jax.sharding import PartitionSpec as P

MESH = pl.DeviceIdType.MESH
B = 128
SKEW = 4


def triangle(rows):
    return [(i, j) for i in range(rows) for j in range(i + 1)]


def kernel(
    n, ng, given, out, mine, before, following, own, from_left, from_right, to_right, to_left,
    kept, to_before, from_next, m_sem, x_send, x_recv, y_send, y_recv, s_send, s_recv,
    r_send, r_recv, l_send, l_recv,
):
    z = lax.axis_index("group")
    g = lax.axis_index("genome")
    samples, width = given.shape
    rows = samples // B
    blocks = triangle(rows)
    first = [i * (i + 1) // 2 for i in range(rows)]
    groups = [(i, 0, i + 1) for i in range(rows - 1)]
    early = list(groups)
    groups += [(rows - 1, 0, rows - 2), (rows - 1, rows - 2, 2)]

    has_left, has_right = z > 0, z < n - 1
    has_before, has_next = g > 0, g < ng - 1

    barrier = pltpu.get_barrier_semaphore()

    def greet(there, where):
        @pl.when(there)
        def _():
            pl.semaphore_signal(barrier, inc=1, device_id=where, device_id_type=MESH)

    greet(has_left, {"group": z - 1})
    greet(has_right, {"group": z + 1})
    greet(has_before, {"genome": g - 1})
    greet(has_next, {"genome": g + 1})

    def load(i):
        span = pl.ds(i * B, B)
        return pltpu.make_async_copy(given.at[span], mine.at[span], m_sem.at[i])

    for i in range(rows):
        load(i).start()

    peers = jnp.minimum(z, 1) + jnp.minimum(n - 1 - z, 1)
    peers = peers + jnp.minimum(g, 1) + jnp.minimum(ng - 1 - g, 1)
    pl.semaphore_wait(barrier, peers)

    def row_copy(i):
        span = pl.ds(i * B, B)
        return pltpu.make_async_remote_copy(
            src_ref=mine.at[span],
            dst_ref=before.at[span],
            send_sem=x_send.at[i],
            recv_sem=x_recv.at[i],
            device_id={"genome": g + 1},
            device_id_type=MESH,
        )

    def follower_copy(i):
        span = pl.ds(i * B, B)
        return pltpu.make_async_remote_copy(
            src_ref=mine.at[span],
            dst_ref=following.at[span],
            send_sem=y_send.at[i],
            recv_sem=y_recv.at[i],
            device_id={"genome": g - 1},
            device_id_type=MESH,
        )

    def score_copy():
        return pltpu.make_async_remote_copy(
            src_ref=to_before,
            dst_ref=from_next,
            send_sem=s_send,
            recv_sem=s_recv,
            device_id={"genome": g - 1},
            device_id_type=MESH,
        )

    def right_copy(c):
        return pltpu.make_async_remote_copy(
            src_ref=to_right.at[c],
            dst_ref=from_left.at[c],
            send_sem=r_send.at[c],
            recv_sem=r_recv.at[c],
            device_id={"group": z + 1},
            device_id_type=MESH,
        )

    def left_copy(c):
        return pltpu.make_async_remote_copy(
            src_ref=to_left.at[c],
            dst_ref=from_right.at[c],
            send_sem=l_send.at[c],
            recv_sem=l_recv.at[c],
            device_id={"group": z - 1},
            device_id_type=MESH,
        )

    def products(ref, i, add):
        band = lax.dot_general(
            ref[pl.ds(i * B, B), :],
            ref[pl.ds(0, (i + 1) * B), :],
            (((1,), (1,)), ((), ())),
            preferred_element_type=jnp.float32,
        )
        for j in range(i + 1):
            block = band[:, j * B : (j + 1) * B]
            own[first[i] + j] = own[first[i] + j] + block if add else block

    def scored(group, returned, here):
        i, j, count = group
        parts = []
        for k in range(j, j + count):
            part = own[first[i] + k]
            parts.append(part if k == i else part + part)
        whole = jnp.concatenate(parts, axis=1) if count > 1 else parts[0]
        high = whole.astype(jnp.bfloat16)
        low = (whole - high.astype(jnp.float32)).astype(jnp.bfloat16)
        both = jnp.concatenate([high, low], axis=0)

        def add(total, ref):
            product = lax.dot_general(
                both,
                ref[pl.ds(j * B, count * B), :],
                (((1,), (0,)), ((), ())),
                preferred_element_type=jnp.float32,
            )
            weighed = (product[:B] + product[B:]) * ref[pl.ds(i * B, B), :].astype(
                jnp.float32
            )
            total[...] += jnp.sum(weighed, axis=0, keepdims=True)

        if returned and group in early:

            @pl.when(has_before)
            def _():
                if group == early[0]:
                    for k in range(rows):
                        row_copy(k).wait_recv()
                add(to_before, before)
                if group == early[-1]:
                    score_copy().start()

        if here:
            add(kept, mine)

    for i in range(rows):
        load(i).wait()

    @pl.when(has_before)
    def _():
        for i in range(rows):
            follower_copy(i).start()

    products(mine, 0, False)
    kept[...] = jnp.zeros_like(kept)
    to_before[...] = jnp.zeros_like(to_before)
    pending = list(groups)
    at_end = (z == 0) | (z == n - 1)

    for t in range(len(blocks) + SKEW * (n - 1)):
        if t == first[rows - 1]:

            @pl.when(has_next)
            def _():
                for i in range(rows):
                    follower_copy(i).wait_recv()
                products(following, rows - 1, True)

        c = t - SKEW * z

        @pl.when(has_right & (c >= 0) & (c < len(blocks)))
        def _():
            @pl.when(has_left)
            def _():
                right_copy(c).wait_recv()
                total = own[c] + from_left[c].astype(jnp.float32)
                to_right[c] = total.astype(to_right.dtype)

            @pl.when(z == 0)
            def _():
                to_right[c] = own[c].astype(to_right.dtype)

            right_copy(c).start()

        d = t - SKEW * (n - 1 - z)

        @pl.when(has_left & (d >= 0) & (d < len(blocks)))
        def _():
            @pl.when(has_right)
            def _():
                left_copy(d).wait_recv()
                total = own[d] + from_right[d].astype(jnp.float32)
                to_left[d] = total.astype(to_left.dtype)

            @pl.when(z == n - 1)
            def _():
                to_left[d] = own[d].astype(to_left.dtype)

            left_copy(d).start()

        if t in first[: rows - 1]:
            products(mine, first.index(t) + 1, False)

        if t == 4:

            @pl.when(has_next)
            def _():
                for i in range(rows):
                    row_copy(i).start()

        f = t - SKEW * jnp.maximum(z, n - 1 - z)

        @pl.when((f >= 0) & (f < len(blocks)))
        def _():
            @pl.when(has_left)
            def _():
                @pl.when(z == n - 1)
                def _():
                    right_copy(f).wait_recv()

                own[f] = own[f] + from_left[f].astype(jnp.float32)

            @pl.when(has_right)
            def _():
                @pl.when(z == 0)
                def _():
                    left_copy(f).wait_recv()

                own[f] = own[f] + from_right[f].astype(jnp.float32)

        ready = t - SKEW * (n - 1)
        group = pending[0]
        if ready == first[group[0]] + group[1] + group[2] - 1:

            @pl.when(at_end)
            def _():
                scored(group, True, True)

            pending.pop(0)

    @pl.when(jnp.logical_not(at_end))
    def _():
        for group in early:
            scored(group, True, False)
        for group in groups:
            scored(group, False, True)

    @pl.when(has_next)
    def _():
        score_copy().wait_recv()
        kept[...] += from_next[...]

    out[...] = kept[...] * (1.0 / samples) * (1.0 / samples)

    @pl.when(has_next)
    def _():
        for i in range(rows):
            row_copy(i).wait_send()

    @pl.when(has_before)
    def _():
        score_copy().wait_send()
        for i in range(rows):
            follower_copy(i).wait_send()

    @pl.when(has_right)
    def _():
        for c in range(len(blocks)):
            right_copy(c).wait_send()

    @pl.when(has_left)
    def _():
        for c in range(len(blocks)):
            left_copy(c).wait_send()


def solution(mesh):
    n, ng = mesh.shape["group"], mesh.shape["genome"]

    def per_device(genotypes):
        samples, width = genotypes.shape
        rows = samples // B
        steps = len(triangle(rows))
        sent = pltpu.VMEM((steps, B, B), jnp.bfloat16)
        line = pltpu.VMEM((1, width), jnp.float32)
        scores = pl.pallas_call(
            functools.partial(kernel, n, ng),
            out_shape=jax.ShapeDtypeStruct((1, width), jnp.float32),
            in_specs=[pl.BlockSpec(memory_space=pl.ANY)],
            out_specs=pl.BlockSpec(memory_space=pltpu.VMEM),
            scratch_shapes=[
                pltpu.VMEM((samples, width), jnp.bfloat16),
                pltpu.VMEM((samples, width), jnp.bfloat16),
                pltpu.VMEM((samples, width), jnp.bfloat16),
                pltpu.VMEM((steps, B, B), jnp.float32),
                sent,
                sent,
                sent,
                sent,
                line,
                line,
                line,
                pltpu.SemaphoreType.DMA((rows,)),
                pltpu.SemaphoreType.DMA((rows,)),
                pltpu.SemaphoreType.DMA((rows,)),
                pltpu.SemaphoreType.DMA((rows,)),
                pltpu.SemaphoreType.DMA((rows,)),
                pltpu.SemaphoreType.DMA,
                pltpu.SemaphoreType.DMA,
                pltpu.SemaphoreType.DMA((steps,)),
                pltpu.SemaphoreType.DMA((steps,)),
                pltpu.SemaphoreType.DMA((steps,)),
                pltpu.SemaphoreType.DMA((steps,)),
            ],
            compiler_params=pltpu.CompilerParams(
                collective_id=0,
                has_side_effects=True,
                vmem_limit_bytes=54784 * 1024,
            ),
        )(genotypes)
        return scores.reshape(width)

    return jax.shard_map(
        per_device,
        mesh=mesh,
        in_specs=(P(None, ("slab", "genome", "group")),),
        out_specs=P(("slab", "genome", "group")),
        check_vma=False,
    )
```

```python
import functools

import jax
import jax.numpy as jnp
from jax import lax
from jax.experimental import pallas as pl
from jax.experimental.pallas import tpu as pltpu
from jax.sharding import PartitionSpec as P

MESH = pl.DeviceIdType.MESH
B = 128
SKEW = 4


def triangle(rows):
    return [(i, j) for i in range(rows) for j in range(i + 1)]


def kernel(
    n, ng, given, out, mine, before, following, own, from_left, from_right, to_right, to_left,
    kept, to_before, from_next, m_sem, x_send, x_recv, y_send, y_recv, s_send, s_recv,
    r_send, r_recv, l_send, l_recv,
):
    z = lax.axis_index("group")
    g = lax.axis_index("genome")
    samples, width = given.shape
    rows = samples // B
    blocks = triangle(rows)
    first = [i * (i + 1) // 2 for i in range(rows)]
    groups = [(i, 0, i + 1) for i in range(rows - 1)] + [(rows - 1, 0, rows - 3)]
    early = list(groups)
    late = (rows - 1, rows - 3, 3)
    groups.append(late)
    late_step = first[rows - 1] + late[1]

    has_left, has_right = z > 0, z < n - 1
    has_before, has_next = g > 0, g < ng - 1

    barrier = pltpu.get_barrier_semaphore()

    def greet(there, where):
        @pl.when(there)
        def _():
            pl.semaphore_signal(barrier, inc=1, device_id=where, device_id_type=MESH)

    greet(has_left, {"group": z - 1})
    greet(has_right, {"group": z + 1})
    greet(has_before, {"genome": g - 1})
    greet(has_next, {"genome": g + 1})

    def load(i):
        span = pl.ds(i * B, B)
        return pltpu.make_async_copy(given.at[span], mine.at[span], m_sem.at[i])

    for i in range(rows):
        load(i).start()

    def products(ref, group, add):
        i, low, count = group
        band = lax.dot_general(
            ref[pl.ds(i * B, B), :],
            ref[pl.ds(low * B, count * B), :],
            (((1,), (1,)), ((), ())),
            preferred_element_type=jnp.float32,
        )
        for k in range(count):
            b = first[i] + low + k
            block = band[:, k * B : (k + 1) * B]
            own[b] = own[b] + block if add else block

    for i in range(2):
        load(i).wait()
        products(mine, (i, 0, i + 1), False)

    peers = jnp.minimum(z, 1) + jnp.minimum(n - 1 - z, 1)
    peers = peers + jnp.minimum(g, 1) + jnp.minimum(ng - 1 - g, 1)
    pl.semaphore_wait(barrier, peers)

    def row_copy(i):
        span = pl.ds(i * B, B)
        return pltpu.make_async_remote_copy(
            src_ref=mine.at[span],
            dst_ref=before.at[span],
            send_sem=x_send.at[i],
            recv_sem=x_recv.at[i],
            device_id={"genome": g + 1},
            device_id_type=MESH,
        )

    def follower_copy(i):
        span = pl.ds(i * B, B)
        return pltpu.make_async_remote_copy(
            src_ref=mine.at[span],
            dst_ref=following.at[span],
            send_sem=y_send.at[i],
            recv_sem=y_recv.at[i],
            device_id={"genome": g - 1},
            device_id_type=MESH,
        )

    def score_copy():
        return pltpu.make_async_remote_copy(
            src_ref=to_before,
            dst_ref=from_next,
            send_sem=s_send,
            recv_sem=s_recv,
            device_id={"genome": g - 1},
            device_id_type=MESH,
        )

    def right_copy(c):
        return pltpu.make_async_remote_copy(
            src_ref=to_right.at[c],
            dst_ref=from_left.at[c],
            send_sem=r_send.at[c],
            recv_sem=r_recv.at[c],
            device_id={"group": z + 1},
            device_id_type=MESH,
        )

    def left_copy(c):
        return pltpu.make_async_remote_copy(
            src_ref=to_left.at[c],
            dst_ref=from_right.at[c],
            send_sem=l_send.at[c],
            recv_sem=l_recv.at[c],
            device_id={"group": z - 1},
            device_id_type=MESH,
        )

    def scored(group, returned, here):
        i, j, count = group
        parts = []
        for k in range(j, j + count):
            part = own[first[i] + k]
            parts.append(part if k == i else part + part)
        whole = jnp.concatenate(parts, axis=1) if count > 1 else parts[0]
        high = whole.astype(jnp.bfloat16)
        low = (whole - high.astype(jnp.float32)).astype(jnp.bfloat16)
        both = jnp.concatenate([high, low], axis=0)

        def add(total, ref):
            product = lax.dot_general(
                both,
                ref[pl.ds(j * B, count * B), :],
                (((1,), (0,)), ((), ())),
                preferred_element_type=jnp.float32,
            )
            weighed = (product[:B] + product[B:]) * ref[pl.ds(i * B, B), :].astype(
                jnp.float32
            )
            total[...] += jnp.sum(weighed, axis=0, keepdims=True)

        if returned and group in early:

            @pl.when(has_before)
            def _():
                if group == early[0]:
                    for k in range(rows):
                        row_copy(k).wait_recv()
                add(to_before, before)
                if group == early[-1]:
                    score_copy().start()

        if here:
            add(kept, mine)

    for i in range(2, rows):
        load(i).wait()

    @pl.when(has_before)
    def _():
        for i in range(late[1], rows):
            follower_copy(i).start()

    kept[...] = jnp.zeros_like(kept)
    to_before[...] = jnp.zeros_like(to_before)
    pending = list(groups)
    at_end = (z == 0) | (z == n - 1)

    for t in range(len(blocks) + SKEW * (n - 1)):
        inner = (t - late_step) // SKEW
        if t >= late_step and (t - late_step) % SKEW == 0 and inner <= (n - 1) // 2:

            @pl.when(has_next & (jnp.minimum(z, n - 1 - z) == inner))
            def _():
                for i in range(late[1], rows):
                    follower_copy(i).wait_recv()
                products(following, late, True)

        c = t - SKEW * z

        @pl.when(has_right & (c >= 0) & (c < len(blocks)))
        def _():
            @pl.when(has_left)
            def _():
                right_copy(c).wait_recv()
                total = own[c] + from_left[c].astype(jnp.float32)
                to_right[c] = total.astype(to_right.dtype)

            @pl.when(z == 0)
            def _():
                to_right[c] = own[c].astype(to_right.dtype)

            right_copy(c).start()

        d = t - SKEW * (n - 1 - z)

        @pl.when(has_left & (d >= 0) & (d < len(blocks)))
        def _():
            @pl.when(has_right)
            def _():
                left_copy(d).wait_recv()
                total = own[d] + from_right[d].astype(jnp.float32)
                to_left[d] = total.astype(to_left.dtype)

            @pl.when(z == n - 1)
            def _():
                to_left[d] = own[d].astype(to_left.dtype)

            left_copy(d).start()

        if t in first[1 : rows - 1]:
            i = first.index(t) + 1
            products(mine, (i, 0, i + 1), False)

        if t == 2:

            @pl.when(has_next)
            def _():
                for i in range(rows):
                    row_copy(i).start()

        f = t - SKEW * jnp.maximum(z, n - 1 - z)

        @pl.when((f >= 0) & (f < len(blocks)))
        def _():
            @pl.when(has_left)
            def _():
                @pl.when(z == n - 1)
                def _():
                    right_copy(f).wait_recv()

                own[f] = own[f] + from_left[f].astype(jnp.float32)

            @pl.when(has_right)
            def _():
                @pl.when(z == 0)
                def _():
                    left_copy(f).wait_recv()

                own[f] = own[f] + from_right[f].astype(jnp.float32)

        ready = t - SKEW * (n - 1)
        group = pending[0]
        if ready == first[group[0]] + group[1] + group[2] - 1:

            @pl.when(at_end)
            def _():
                scored(group, True, True)

            if group[0] < rows - 2:

                @pl.when(jnp.logical_not(at_end))
                def _():
                    scored(group, True, False)

            pending.pop(0)

    @pl.when(jnp.logical_not(at_end))
    def _():
        for group in early:
            if group[0] >= rows - 2:
                scored(group, True, False)
        for group in groups:
            scored(group, False, True)

    @pl.when(has_next)
    def _():
        score_copy().wait_recv()
        kept[...] += from_next[...]

    out[...] = kept[...] * (1.0 / samples) * (1.0 / samples)

    @pl.when(has_next)
    def _():
        for i in range(rows):
            row_copy(i).wait_send()

    @pl.when(has_before)
    def _():
        score_copy().wait_send()
        for i in range(late[1], rows):
            follower_copy(i).wait_send()

    @pl.when(has_right)
    def _():
        for c in range(len(blocks)):
            right_copy(c).wait_send()

    @pl.when(has_left)
    def _():
        for c in range(len(blocks)):
            left_copy(c).wait_send()


def solution(mesh):
    n, ng = mesh.shape["group"], mesh.shape["genome"]

    def per_device(genotypes):
        samples, width = genotypes.shape
        rows = samples // B
        steps = len(triangle(rows))
        sent = pltpu.VMEM((steps, B, B), jnp.bfloat16)
        line = pltpu.VMEM((1, width), jnp.float32)
        scores = pl.pallas_call(
            functools.partial(kernel, n, ng),
            out_shape=jax.ShapeDtypeStruct((1, width), jnp.float32),
            in_specs=[pl.BlockSpec(memory_space=pl.ANY)],
            out_specs=pl.BlockSpec(memory_space=pltpu.VMEM),
            scratch_shapes=[
                pltpu.VMEM((samples, width), jnp.bfloat16),
                pltpu.VMEM((samples, width), jnp.bfloat16),
                pltpu.VMEM((samples, width), jnp.bfloat16),
                pltpu.VMEM((steps, B, B), jnp.float32),
                sent,
                sent,
                sent,
                sent,
                line,
                line,
                line,
                pltpu.SemaphoreType.DMA((rows,)),
                pltpu.SemaphoreType.DMA((rows,)),
                pltpu.SemaphoreType.DMA((rows,)),
                pltpu.SemaphoreType.DMA((rows,)),
                pltpu.SemaphoreType.DMA((rows,)),
                pltpu.SemaphoreType.DMA,
                pltpu.SemaphoreType.DMA,
                pltpu.SemaphoreType.DMA((steps,)),
                pltpu.SemaphoreType.DMA((steps,)),
                pltpu.SemaphoreType.DMA((steps,)),
                pltpu.SemaphoreType.DMA((steps,)),
            ],
            compiler_params=pltpu.CompilerParams(
                collective_id=0,
                has_side_effects=True,
                vmem_limit_bytes=54784 * 1024,
            ),
        )(genotypes)
        return scores.reshape(width)

    return jax.shard_map(
        per_device,
        mesh=mesh,
        in_specs=(P(None, ("slab", "genome", "group")),),
        out_specs=P(("slab", "genome", "group")),
        check_vma=False,
    )
```

```python
import functools

import jax
import jax.numpy as jnp
from jax import lax
from jax.experimental import pallas as pl
from jax.experimental.pallas import tpu as pltpu
from jax.sharding import PartitionSpec as P

MESH = pl.DeviceIdType.MESH
B = 128
SKEW = 4


def triangle(rows):
    return [(i, j) for i in range(rows) for j in range(i + 1)]


def kernel(
    n, ng, given, out, mine, before, following, own, from_left, from_right, to_right, to_left,
    kept, to_before, from_next, m_sem, x_send, x_recv, y_send, y_recv, s_send, s_recv,
    r_send, r_recv, l_send, l_recv,
):
    z = lax.axis_index("group")
    g = lax.axis_index("genome")
    samples, width = given.shape
    rows = samples // B
    blocks = triangle(rows)
    first = [i * (i + 1) // 2 for i in range(rows)]
    groups = [(i, 0, i + 1) for i in range(rows - 1)] + [(rows - 1, 0, rows - 3)]
    early = list(groups)
    late = (rows - 1, rows - 3, 3)
    groups.append(late)
    late_step = first[rows - 1] + late[1]

    has_left, has_right = z > 0, z < n - 1
    has_before, has_next = g > 0, g < ng - 1

    barrier = pltpu.get_barrier_semaphore()

    def greet(there, where):
        @pl.when(there)
        def _():
            pl.semaphore_signal(barrier, inc=1, device_id=where, device_id_type=MESH)

    greet(has_left, {"group": z - 1})
    greet(has_right, {"group": z + 1})
    greet(has_before, {"genome": g - 1})
    greet(has_next, {"genome": g + 1})

    def load(i):
        span = pl.ds(i * B, B)
        return pltpu.make_async_copy(given.at[span], mine.at[span], m_sem.at[i])

    for i in range(rows):
        load(i).start()

    def products(ref, group, add):
        i, low, count = group
        band = lax.dot_general(
            ref[pl.ds(i * B, B), :],
            ref[pl.ds(low * B, count * B), :],
            (((1,), (1,)), ((), ())),
            preferred_element_type=jnp.float32,
        )
        for k in range(count):
            b = first[i] + low + k
            block = band[:, k * B : (k + 1) * B]
            own[b] = own[b] + block if add else block

    for i in range(2):
        load(i).wait()
        products(mine, (i, 0, i + 1), False)

    peers = jnp.minimum(z, 1) + jnp.minimum(n - 1 - z, 1)
    peers = peers + jnp.minimum(g, 1) + jnp.minimum(ng - 1 - g, 1)
    pl.semaphore_wait(barrier, peers)

    def row_copy(i):
        span = pl.ds(i * B, B)
        return pltpu.make_async_remote_copy(
            src_ref=mine.at[span],
            dst_ref=before.at[span],
            send_sem=x_send.at[i],
            recv_sem=x_recv.at[i],
            device_id={"genome": g + 1},
            device_id_type=MESH,
        )

    def follower_copy(i):
        span = pl.ds(i * B, B)
        return pltpu.make_async_remote_copy(
            src_ref=mine.at[span],
            dst_ref=following.at[span],
            send_sem=y_send.at[i],
            recv_sem=y_recv.at[i],
            device_id={"genome": g - 1},
            device_id_type=MESH,
        )

    def score_copy():
        return pltpu.make_async_remote_copy(
            src_ref=to_before,
            dst_ref=from_next,
            send_sem=s_send,
            recv_sem=s_recv,
            device_id={"genome": g - 1},
            device_id_type=MESH,
        )

    def right_copy(c):
        return pltpu.make_async_remote_copy(
            src_ref=to_right.at[c],
            dst_ref=from_left.at[c],
            send_sem=r_send.at[c],
            recv_sem=r_recv.at[c],
            device_id={"group": z + 1},
            device_id_type=MESH,
        )

    def left_copy(c):
        return pltpu.make_async_remote_copy(
            src_ref=to_left.at[c],
            dst_ref=from_right.at[c],
            send_sem=l_send.at[c],
            recv_sem=l_recv.at[c],
            device_id={"group": z - 1},
            device_id_type=MESH,
        )

    def scored(group, returned, here):
        i, j, count = group
        parts = []
        for k in range(j, j + count):
            part = own[first[i] + k]
            parts.append(part if k == i else part + part)
        whole = jnp.concatenate(parts, axis=1) if count > 1 else parts[0]
        high = whole.astype(jnp.bfloat16)
        low = (whole - high.astype(jnp.float32)).astype(jnp.bfloat16)
        both = jnp.concatenate([high, low], axis=0)

        def add(total, ref):
            product = lax.dot_general(
                both,
                ref[pl.ds(j * B, count * B), :],
                (((1,), (0,)), ((), ())),
                preferred_element_type=jnp.float32,
            )
            weighed = (product[:B] + product[B:]) * ref[pl.ds(i * B, B), :].astype(
                jnp.float32
            )
            total[...] += jnp.sum(weighed, axis=0, keepdims=True)

        if returned and group in early:

            @pl.when(has_before)
            def _():
                if group == early[0]:
                    for k in range(rows):
                        row_copy(k).wait_recv()
                add(to_before, before)
                if group == early[-1]:
                    score_copy().start()

        if here:
            add(kept, mine)

    kept[...] = jnp.zeros_like(kept)
    to_before[...] = jnp.zeros_like(to_before)
    pending = list(groups)
    at_end = (z == 0) | (z == n - 1)

    for t in range(len(blocks) + SKEW * (n - 1)):
        inner = (t - late_step) // SKEW
        if t >= late_step and (t - late_step) % SKEW == 0 and inner <= (n - 1) // 2:

            @pl.when(has_next & (jnp.minimum(z, n - 1 - z) == inner))
            def _():
                for i in range(late[1], rows):
                    follower_copy(i).wait_recv()
                products(following, late, True)

        d = t - SKEW * (n - 1 - z)

        @pl.when(has_left & (d >= 0) & (d < len(blocks)))
        def _():
            @pl.when(has_right)
            def _():
                left_copy(d).wait_recv()
                total = own[d] + from_right[d].astype(jnp.float32)
                to_left[d] = total.astype(to_left.dtype)

            @pl.when(z == n - 1)
            def _():
                to_left[d] = own[d].astype(to_left.dtype)

            left_copy(d).start()

        c = t - SKEW * z

        @pl.when(has_right & (c >= 0) & (c < len(blocks)))
        def _():
            @pl.when(has_left)
            def _():
                right_copy(c).wait_recv()
                total = own[c] + from_left[c].astype(jnp.float32)
                to_right[c] = total.astype(to_right.dtype)

            @pl.when(z == 0)
            def _():
                to_right[c] = own[c].astype(to_right.dtype)

            right_copy(c).start()

        if t == 0:
            for i in range(2, rows):
                load(i).wait()

            @pl.when(has_before)
            def _():
                for i in range(late[1], rows):
                    follower_copy(i).start()

        if t in first[1 : rows - 1]:
            i = first.index(t) + 1
            products(mine, (i, 0, i + 1), False)

        if t == 2:

            @pl.when(has_next)
            def _():
                for i in range(rows):
                    row_copy(i).start()

        f = t - SKEW * jnp.maximum(z, n - 1 - z)

        @pl.when((f >= 0) & (f < len(blocks)))
        def _():
            @pl.when(has_left)
            def _():
                @pl.when(z == n - 1)
                def _():
                    right_copy(f).wait_recv()

                own[f] = own[f] + from_left[f].astype(jnp.float32)

            @pl.when(has_right)
            def _():
                @pl.when(z == 0)
                def _():
                    left_copy(f).wait_recv()

                own[f] = own[f] + from_right[f].astype(jnp.float32)

        ready = t - SKEW * (n - 1)
        group = pending[0]
        if ready == first[group[0]] + group[1] + group[2] - 1:

            @pl.when(at_end)
            def _():
                scored(group, True, True)

            if group[0] < rows - 2:

                @pl.when(jnp.logical_not(at_end))
                def _():
                    scored(group, True, False)

            pending.pop(0)

    @pl.when(jnp.logical_not(at_end))
    def _():
        for group in early:
            if group[0] >= rows - 2:
                scored(group, True, False)
        for group in groups:
            scored(group, False, True)

    @pl.when(has_next)
    def _():
        score_copy().wait_recv()
        kept[...] += from_next[...]

    out[...] = kept[...] * (1.0 / samples) * (1.0 / samples)

    @pl.when(has_next)
    def _():
        for i in range(rows):
            row_copy(i).wait_send()

    @pl.when(has_before)
    def _():
        score_copy().wait_send()
        for i in range(late[1], rows):
            follower_copy(i).wait_send()

    @pl.when(has_right)
    def _():
        for c in range(len(blocks)):
            right_copy(c).wait_send()

    @pl.when(has_left)
    def _():
        for c in range(len(blocks)):
            left_copy(c).wait_send()


def solution(mesh):
    n, ng = mesh.shape["group"], mesh.shape["genome"]

    def per_device(genotypes):
        samples, width = genotypes.shape
        rows = samples // B
        steps = len(triangle(rows))
        sent = pltpu.VMEM((steps, B, B), jnp.bfloat16)
        line = pltpu.VMEM((1, width), jnp.float32)
        scores = pl.pallas_call(
            functools.partial(kernel, n, ng),
            out_shape=jax.ShapeDtypeStruct((1, width), jnp.float32),
            in_specs=[pl.BlockSpec(memory_space=pl.ANY)],
            out_specs=pl.BlockSpec(memory_space=pltpu.VMEM),
            scratch_shapes=[
                pltpu.VMEM((samples, width), jnp.bfloat16),
                pltpu.VMEM((samples, width), jnp.bfloat16),
                pltpu.VMEM((samples, width), jnp.bfloat16),
                pltpu.VMEM((steps, B, B), jnp.float32),
                sent,
                sent,
                sent,
                sent,
                line,
                line,
                line,
                pltpu.SemaphoreType.DMA((rows,)),
                pltpu.SemaphoreType.DMA((rows,)),
                pltpu.SemaphoreType.DMA((rows,)),
                pltpu.SemaphoreType.DMA((rows,)),
                pltpu.SemaphoreType.DMA((rows,)),
                pltpu.SemaphoreType.DMA,
                pltpu.SemaphoreType.DMA,
                pltpu.SemaphoreType.DMA((steps,)),
                pltpu.SemaphoreType.DMA((steps,)),
                pltpu.SemaphoreType.DMA((steps,)),
                pltpu.SemaphoreType.DMA((steps,)),
            ],
            compiler_params=pltpu.CompilerParams(
                collective_id=0,
                has_side_effects=True,
                vmem_limit_bytes=54784 * 1024,
            ),
        )(genotypes)
        return scores.reshape(width)

    return jax.shard_map(
        per_device,
        mesh=mesh,
        in_specs=(P(None, ("slab", "genome", "group")),),
        out_specs=P(("slab", "genome", "group")),
        check_vma=False,
    )
```

```python
import functools

import jax
import jax.numpy as jnp
from jax import lax
from jax.experimental import pallas as pl
from jax.experimental.pallas import tpu as pltpu
from jax.sharding import PartitionSpec as P

MESH = pl.DeviceIdType.MESH
B = 128
SKEW = 4


def triangle(rows):
    return [(i, j) for i in range(rows) for j in range(i + 1)]


def kernel(
    n, ng, given, out, mine, before, following, own, from_left, from_right, to_right, to_left,
    kept, to_before, from_next, m_sem, x_send, x_recv, y_send, y_recv, s_send, s_recv,
    r_send, r_recv, l_send, l_recv,
):
    z = lax.axis_index("group")
    g = lax.axis_index("genome")
    samples, width = given.shape
    rows = samples // B
    blocks = triangle(rows)
    first = [i * (i + 1) // 2 for i in range(rows)]
    groups = [(i, 0, i + 1) for i in range(rows - 1)]
    early = list(groups)
    late = (rows - 1, 0, rows)
    groups += [(rows - 1, 0, rows - 2), (rows - 1, rows - 2, 2)]
    late_step = first[rows - 1] + late[1]

    has_left, has_right = z > 0, z < n - 1
    has_before, has_next = g > 0, g < ng - 1

    barrier = pltpu.get_barrier_semaphore()

    def greet(there, where):
        @pl.when(there)
        def _():
            pl.semaphore_signal(barrier, inc=1, device_id=where, device_id_type=MESH)

    greet(has_left, {"group": z - 1})
    greet(has_right, {"group": z + 1})
    greet(has_before, {"genome": g - 1})
    greet(has_next, {"genome": g + 1})

    def load(i):
        span = pl.ds(i * B, B)
        return pltpu.make_async_copy(given.at[span], mine.at[span], m_sem.at[i])

    for i in range(rows):
        load(i).start()

    def products(ref, group, add):
        i, low, count = group
        band = lax.dot_general(
            ref[pl.ds(i * B, B), :],
            ref[pl.ds(low * B, count * B), :],
            (((1,), (1,)), ((), ())),
            preferred_element_type=jnp.float32,
        )
        for k in range(count):
            b = first[i] + low + k
            block = band[:, k * B : (k + 1) * B]
            own[b] = own[b] + block if add else block

    for i in range(2):
        load(i).wait()
        products(mine, (i, 0, i + 1), False)

    peers = jnp.minimum(z, 1) + jnp.minimum(n - 1 - z, 1)
    peers = peers + jnp.minimum(g, 1) + jnp.minimum(ng - 1 - g, 1)
    pl.semaphore_wait(barrier, peers)

    def row_copy(i):
        span = pl.ds(i * B, B)
        return pltpu.make_async_remote_copy(
            src_ref=mine.at[span],
            dst_ref=before.at[span],
            send_sem=x_send.at[i],
            recv_sem=x_recv.at[i],
            device_id={"genome": g + 1},
            device_id_type=MESH,
        )

    def follower_copy(i):
        span = pl.ds(i * B, B)
        return pltpu.make_async_remote_copy(
            src_ref=mine.at[span],
            dst_ref=following.at[span],
            send_sem=y_send.at[i],
            recv_sem=y_recv.at[i],
            device_id={"genome": g - 1},
            device_id_type=MESH,
        )

    def score_copy():
        return pltpu.make_async_remote_copy(
            src_ref=to_before,
            dst_ref=from_next,
            send_sem=s_send,
            recv_sem=s_recv,
            device_id={"genome": g - 1},
            device_id_type=MESH,
        )

    def right_copy(c):
        return pltpu.make_async_remote_copy(
            src_ref=to_right.at[c],
            dst_ref=from_left.at[c],
            send_sem=r_send.at[c],
            recv_sem=r_recv.at[c],
            device_id={"group": z + 1},
            device_id_type=MESH,
        )

    def left_copy(c):
        return pltpu.make_async_remote_copy(
            src_ref=to_left.at[c],
            dst_ref=from_right.at[c],
            send_sem=l_send.at[c],
            recv_sem=l_recv.at[c],
            device_id={"group": z - 1},
            device_id_type=MESH,
        )

    def scored(group, returned, here):
        i, j, count = group
        parts = []
        for k in range(j, j + count):
            part = own[first[i] + k]
            parts.append(part if k == i else part + part)
        whole = jnp.concatenate(parts, axis=1) if count > 1 else parts[0]
        high = whole.astype(jnp.bfloat16)
        low = (whole - high.astype(jnp.float32)).astype(jnp.bfloat16)
        both = jnp.concatenate([high, low], axis=0)

        def add(total, ref):
            product = lax.dot_general(
                both,
                ref[pl.ds(j * B, count * B), :],
                (((1,), (0,)), ((), ())),
                preferred_element_type=jnp.float32,
            )
            weighed = (product[:B] + product[B:]) * ref[pl.ds(i * B, B), :].astype(
                jnp.float32
            )
            total[...] += jnp.sum(weighed, axis=0, keepdims=True)

        if returned and group in early:

            @pl.when(has_before)
            def _():
                if group == early[0]:
                    for k in range(rows):
                        row_copy(k).wait_recv()
                add(to_before, before)
                if group == early[-1]:
                    score_copy().start()

        if here:
            add(kept, mine)

    kept[...] = jnp.zeros_like(kept)
    to_before[...] = jnp.zeros_like(to_before)
    pending = list(groups)
    at_end = (z == 0) | (z == n - 1)

    for t in range(len(blocks) + SKEW * (n - 1)):
        inner = (t - late_step) // SKEW
        if t >= late_step and (t - late_step) % SKEW == 0 and inner <= (n - 1) // 2:

            @pl.when(has_next & (jnp.minimum(z, n - 1 - z) == inner))
            def _():
                for i in range(late[1], rows):
                    follower_copy(i).wait_recv()
                products(following, late, True)

        d = t - SKEW * (n - 1 - z)

        @pl.when(has_left & (d >= 0) & (d < len(blocks)))
        def _():
            @pl.when(has_right)
            def _():
                left_copy(d).wait_recv()
                total = own[d] + from_right[d].astype(jnp.float32)
                to_left[d] = total.astype(to_left.dtype)

            @pl.when(z == n - 1)
            def _():
                to_left[d] = own[d].astype(to_left.dtype)

            left_copy(d).start()

        c = t - SKEW * z

        @pl.when(has_right & (c >= 0) & (c < len(blocks)))
        def _():
            @pl.when(has_left)
            def _():
                right_copy(c).wait_recv()
                total = own[c] + from_left[c].astype(jnp.float32)
                to_right[c] = total.astype(to_right.dtype)

            @pl.when(z == 0)
            def _():
                to_right[c] = own[c].astype(to_right.dtype)

            right_copy(c).start()

        if t == 0:
            for i in range(2, rows):
                load(i).wait()

            @pl.when(has_before)
            def _():
                for i in range(late[1], rows):
                    follower_copy(i).start()

        if t in first[1 : rows - 1]:
            i = first.index(t) + 1
            products(mine, (i, 0, i + 1), False)

        if t == 2:

            @pl.when(has_next)
            def _():
                for i in range(rows):
                    row_copy(i).start()

        f = t - SKEW * jnp.maximum(z, n - 1 - z)

        @pl.when((f >= 0) & (f < len(blocks)))
        def _():
            @pl.when(has_left)
            def _():
                @pl.when(z == n - 1)
                def _():
                    right_copy(f).wait_recv()

                own[f] = own[f] + from_left[f].astype(jnp.float32)

            @pl.when(has_right)
            def _():
                @pl.when(z == 0)
                def _():
                    left_copy(f).wait_recv()

                own[f] = own[f] + from_right[f].astype(jnp.float32)

        ready = t - SKEW * (n - 1)
        group = pending[0]
        if ready == first[group[0]] + group[1] + group[2] - 1:

            @pl.when(at_end)
            def _():
                scored(group, True, True)

            if group[0] < rows - 2:

                @pl.when(jnp.logical_not(at_end))
                def _():
                    scored(group, True, False)

            pending.pop(0)

    @pl.when(jnp.logical_not(at_end))
    def _():
        for group in early:
            if group[0] >= rows - 2:
                scored(group, True, False)
        for group in groups:
            scored(group, False, True)

    @pl.when(has_next)
    def _():
        score_copy().wait_recv()
        kept[...] += from_next[...]

    out[...] = kept[...] * (1.0 / samples) * (1.0 / samples)

    @pl.when(has_next)
    def _():
        for i in range(rows):
            row_copy(i).wait_send()

    @pl.when(has_before)
    def _():
        score_copy().wait_send()
        for i in range(late[1], rows):
            follower_copy(i).wait_send()

    @pl.when(has_right)
    def _():
        for c in range(len(blocks)):
            right_copy(c).wait_send()

    @pl.when(has_left)
    def _():
        for c in range(len(blocks)):
            left_copy(c).wait_send()


def solution(mesh):
    n, ng = mesh.shape["group"], mesh.shape["genome"]

    def per_device(genotypes):
        samples, width = genotypes.shape
        rows = samples // B
        steps = len(triangle(rows))
        sent = pltpu.VMEM((steps, B, B), jnp.bfloat16)
        line = pltpu.VMEM((1, width), jnp.float32)
        scores = pl.pallas_call(
            functools.partial(kernel, n, ng),
            out_shape=jax.ShapeDtypeStruct((1, width), jnp.float32),
            in_specs=[pl.BlockSpec(memory_space=pl.ANY)],
            out_specs=pl.BlockSpec(memory_space=pltpu.VMEM),
            scratch_shapes=[
                pltpu.VMEM((samples, width), jnp.bfloat16),
                pltpu.VMEM((samples, width), jnp.bfloat16),
                pltpu.VMEM((samples, width), jnp.bfloat16),
                pltpu.VMEM((steps, B, B), jnp.float32),
                sent,
                sent,
                sent,
                sent,
                line,
                line,
                line,
                pltpu.SemaphoreType.DMA((rows,)),
                pltpu.SemaphoreType.DMA((rows,)),
                pltpu.SemaphoreType.DMA((rows,)),
                pltpu.SemaphoreType.DMA((rows,)),
                pltpu.SemaphoreType.DMA((rows,)),
                pltpu.SemaphoreType.DMA,
                pltpu.SemaphoreType.DMA,
                pltpu.SemaphoreType.DMA((steps,)),
                pltpu.SemaphoreType.DMA((steps,)),
                pltpu.SemaphoreType.DMA((steps,)),
                pltpu.SemaphoreType.DMA((steps,)),
            ],
            compiler_params=pltpu.CompilerParams(
                collective_id=0,
                has_side_effects=True,
                vmem_limit_bytes=54784 * 1024,
            ),
        )(genotypes)
        return scores.reshape(width)

    return jax.shard_map(
        per_device,
        mesh=mesh,
        in_specs=(P(None, ("slab", "genome", "group")),),
        out_specs=P(("slab", "genome", "group")),
        check_vma=False,
    )
```

```python
import functools

import jax
import jax.numpy as jnp
from jax import lax
from jax.experimental import pallas as pl
from jax.experimental.pallas import tpu as pltpu
from jax.sharding import PartitionSpec as P

MESH = pl.DeviceIdType.MESH
B = 128
SKEW = 4


def triangle(rows):
    return [(i, j) for i in range(rows) for j in range(i + 1)]


def kernel(
    n, ng, given, out, mine, before, following, own, from_left, from_right, to_right, to_left,
    kept, to_before, from_next, m_sem, x_send, x_recv, y_send, y_recv, s_send, s_recv,
    r_send, r_recv, l_send, l_recv,
):
    z = lax.axis_index("group")
    g = lax.axis_index("genome")
    samples, width = given.shape
    rows = samples // B
    blocks = triangle(rows)
    first = [i * (i + 1) // 2 for i in range(rows)]
    groups = [(i, 0, i + 1) for i in range(rows - 1)]
    early = list(groups)
    late = (rows - 1, 0, rows)
    groups += [(rows - 1, 0, rows - 2), (rows - 1, rows - 2, 2)]
    late_step = first[rows - 1] + late[1]

    has_left, has_right = z > 0, z < n - 1
    has_before, has_next = g > 0, g < ng - 1

    barrier = pltpu.get_barrier_semaphore()

    def greet(there, where):
        @pl.when(there)
        def _():
            pl.semaphore_signal(barrier, inc=1, device_id=where, device_id_type=MESH)

    greet(has_left, {"group": z - 1})
    greet(has_right, {"group": z + 1})
    greet(has_before, {"genome": g - 1})
    greet(has_next, {"genome": g + 1})

    def load(i):
        span = pl.ds(i * B, B)
        return pltpu.make_async_copy(given.at[span], mine.at[span], m_sem.at[i])

    for i in range(rows):
        load(i).start()

    def products(ref, group, add):
        i, low, count = group
        band = lax.dot_general(
            ref[pl.ds(i * B, B), :],
            ref[pl.ds(low * B, count * B), :],
            (((1,), (1,)), ((), ())),
            preferred_element_type=jnp.float32,
        )
        for k in range(count):
            b = first[i] + low + k
            block = band[:, k * B : (k + 1) * B]
            own[b] = own[b] + block if add else block

    for i in range(2):
        load(i).wait()
        products(mine, (i, 0, i + 1), False)

    peers = jnp.minimum(z, 1) + jnp.minimum(n - 1 - z, 1)
    peers = peers + jnp.minimum(g, 1) + jnp.minimum(ng - 1 - g, 1)
    pl.semaphore_wait(barrier, peers)

    def row_copy(i):
        span = pl.ds(i * B, B)
        return pltpu.make_async_remote_copy(
            src_ref=mine.at[span],
            dst_ref=before.at[span],
            send_sem=x_send.at[i],
            recv_sem=x_recv.at[i],
            device_id={"genome": g + 1},
            device_id_type=MESH,
        )

    def follower_copy(i):
        span = pl.ds(i * B, B)
        return pltpu.make_async_remote_copy(
            src_ref=mine.at[span],
            dst_ref=following.at[span],
            send_sem=y_send.at[i],
            recv_sem=y_recv.at[i],
            device_id={"genome": g - 1},
            device_id_type=MESH,
        )

    def score_copy():
        return pltpu.make_async_remote_copy(
            src_ref=to_before,
            dst_ref=from_next,
            send_sem=s_send,
            recv_sem=s_recv,
            device_id={"genome": g - 1},
            device_id_type=MESH,
        )

    def right_copy(c):
        return pltpu.make_async_remote_copy(
            src_ref=to_right.at[c],
            dst_ref=from_left.at[c],
            send_sem=r_send.at[c],
            recv_sem=r_recv.at[c],
            device_id={"group": z + 1},
            device_id_type=MESH,
        )

    def left_copy(c):
        return pltpu.make_async_remote_copy(
            src_ref=to_left.at[c],
            dst_ref=from_right.at[c],
            send_sem=l_send.at[c],
            recv_sem=l_recv.at[c],
            device_id={"group": z - 1},
            device_id_type=MESH,
        )

    def scored(group, returned, here):
        i, j, count = group
        parts = []
        for k in range(j, j + count):
            part = own[first[i] + k]
            parts.append(part if k == i else part + part)
        whole = jnp.concatenate(parts, axis=1) if count > 1 else parts[0]
        high = whole.astype(jnp.bfloat16)
        low = (whole - high.astype(jnp.float32)).astype(jnp.bfloat16)
        both = jnp.concatenate([high, low], axis=0)

        def add(total, ref):
            product = lax.dot_general(
                both,
                ref[pl.ds(j * B, count * B), :],
                (((1,), (0,)), ((), ())),
                preferred_element_type=jnp.float32,
            )
            weighed = (product[:B] + product[B:]) * ref[pl.ds(i * B, B), :].astype(
                jnp.float32
            )
            total[...] += jnp.sum(weighed, axis=0, keepdims=True)

        if returned and group in early:

            @pl.when(has_before)
            def _():
                if group == early[0]:
                    for k in range(rows):
                        row_copy(k).wait_recv()
                add(to_before, before)
                if group == early[-1]:
                    score_copy().start()

        if here:
            add(kept, mine)

    kept[...] = jnp.zeros_like(kept)
    to_before[...] = jnp.zeros_like(to_before)
    pending = list(groups)
    at_end = (z == 0) | (z == n - 1)

    for t in range(len(blocks) + SKEW * (n - 1)):
        inner = (t - late_step) // SKEW
        if t >= late_step and (t - late_step) % SKEW == 0 and inner <= (n - 1) // 2:

            @pl.when(has_next & (jnp.minimum(z, n - 1 - z) == inner))
            def _():
                for i in range(late[1], rows):
                    follower_copy(i).wait_recv()
                products(following, late, True)

        d = t - SKEW * (n - 1 - z)

        @pl.when(has_left & (d >= 0) & (d < len(blocks)))
        def _():
            @pl.when(has_right)
            def _():
                left_copy(d).wait_recv()
                total = own[d] + from_right[d].astype(jnp.float32)
                to_left[d] = total.astype(to_left.dtype)

            @pl.when(z == n - 1)
            def _():
                to_left[d] = own[d].astype(to_left.dtype)

            left_copy(d).start()

        c = t - SKEW * z

        @pl.when(has_right & (c >= 0) & (c < len(blocks)))
        def _():
            @pl.when(has_left)
            def _():
                right_copy(c).wait_recv()
                total = own[c] + from_left[c].astype(jnp.float32)
                to_right[c] = total.astype(to_right.dtype)

            @pl.when(z == 0)
            def _():
                to_right[c] = own[c].astype(to_right.dtype)

            right_copy(c).start()

        if t == 0:
            for i in range(2, rows):
                load(i).wait()

            @pl.when(has_before)
            def _():
                for i in range(late[1], rows):
                    follower_copy(i).start()

        if t in first[1 : rows - 1]:
            i = first.index(t) + 1
            products(mine, (i, 0, i + 1), False)

        if t == 6:

            @pl.when(has_next)
            def _():
                for i in range(rows):
                    row_copy(i).start()

        f = t - SKEW * jnp.maximum(z, n - 1 - z)

        @pl.when((f >= 0) & (f < len(blocks)))
        def _():
            @pl.when(has_left)
            def _():
                @pl.when(z == n - 1)
                def _():
                    right_copy(f).wait_recv()

                own[f] = own[f] + from_left[f].astype(jnp.float32)

            @pl.when(has_right)
            def _():
                @pl.when(z == 0)
                def _():
                    left_copy(f).wait_recv()

                own[f] = own[f] + from_right[f].astype(jnp.float32)

        ready = t - SKEW * (n - 1)
        group = pending[0]
        if ready == first[group[0]] + group[1] + group[2] - 1:

            @pl.when(at_end)
            def _():
                scored(group, True, True)

            if group[0] < rows - 2:

                @pl.when(jnp.logical_not(at_end))
                def _():
                    scored(group, True, False)

            pending.pop(0)

    @pl.when(jnp.logical_not(at_end))
    def _():
        for group in early:
            if group[0] >= rows - 2:
                scored(group, True, False)
        for group in groups:
            scored(group, False, True)

    @pl.when(has_next)
    def _():
        score_copy().wait_recv()
        kept[...] += from_next[...]

    out[...] = kept[...] * (1.0 / samples) * (1.0 / samples)

    @pl.when(has_next)
    def _():
        for i in range(rows):
            row_copy(i).wait_send()

    @pl.when(has_before)
    def _():
        score_copy().wait_send()
        for i in range(late[1], rows):
            follower_copy(i).wait_send()

    @pl.when(has_right)
    def _():
        for c in range(len(blocks)):
            right_copy(c).wait_send()

    @pl.when(has_left)
    def _():
        for c in range(len(blocks)):
            left_copy(c).wait_send()


def solution(mesh):
    n, ng = mesh.shape["group"], mesh.shape["genome"]

    def per_device(genotypes):
        samples, width = genotypes.shape
        rows = samples // B
        steps = len(triangle(rows))
        sent = pltpu.VMEM((steps, B, B), jnp.bfloat16)
        line = pltpu.VMEM((1, width), jnp.float32)
        scores = pl.pallas_call(
            functools.partial(kernel, n, ng),
            out_shape=jax.ShapeDtypeStruct((1, width), jnp.float32),
            in_specs=[pl.BlockSpec(memory_space=pl.ANY)],
            out_specs=pl.BlockSpec(memory_space=pltpu.VMEM),
            scratch_shapes=[
                pltpu.VMEM((samples, width), jnp.bfloat16),
                pltpu.VMEM((samples, width), jnp.bfloat16),
                pltpu.VMEM((samples, width), jnp.bfloat16),
                pltpu.VMEM((steps, B, B), jnp.float32),
                sent,
                sent,
                sent,
                sent,
                line,
                line,
                line,
                pltpu.SemaphoreType.DMA((rows,)),
                pltpu.SemaphoreType.DMA((rows,)),
                pltpu.SemaphoreType.DMA((rows,)),
                pltpu.SemaphoreType.DMA((rows,)),
                pltpu.SemaphoreType.DMA((rows,)),
                pltpu.SemaphoreType.DMA,
                pltpu.SemaphoreType.DMA,
                pltpu.SemaphoreType.DMA((steps,)),
                pltpu.SemaphoreType.DMA((steps,)),
                pltpu.SemaphoreType.DMA((steps,)),
                pltpu.SemaphoreType.DMA((steps,)),
            ],
            compiler_params=pltpu.CompilerParams(
                collective_id=0,
                has_side_effects=True,
                vmem_limit_bytes=54784 * 1024,
            ),
        )(genotypes)
        return scores.reshape(width)

    return jax.shard_map(
        per_device,
        mesh=mesh,
        in_specs=(P(None, ("slab", "genome", "group")),),
        out_specs=P(("slab", "genome", "group")),
        check_vma=False,
    )
```
